128 devices in a mesh: seq: 32 (over y, z, core), chan: 4 (over x).
Axes of the slice: x: 4, y: 4, z: 4, core: 2. Of those that a mesh axis runs over, the one named last changes fastest.
Arguments:
- projected: bfloat16 [8192, 3, 1024], P('seq', None, 'chan'), may hold values from -6 to 6
- short_taps: float32 [3, 3, 1024], P(None, None, 'chan'), may hold values from -3.5 to 3.5
- filters: float32 [8192, 1024], P('seq', 'chan'), may hold values from -1 to 1, as said below
- skip_gain: float32 [1024], P('chan'), may hold values from -4 to 4
- out_weight: bfloat16 [1024, 1024], P('chan'), may hold values from -0.1875 to 0.1875
Outputs:
- block_out: bfloat16 [8192, 1024], P(('seq', 'chan'))
The draws below stay inside these ranges and needn't reach their ends.
Inputs may be any that keep to these rules, and one draw needn't show every extreme that they name: `filters`: each column is one channel's long filter.
All inputs are finite; a program needn't handle non-finite values.
Results may differ from the reference program's by a relative error of at most 0.018.
Values may be sent and summed in bfloat16 or wider, within the bound.
No kernel may reach another device: no remote copies, remote signals or barrier semaphores. Data moves between devices by JAX's collectives and lax.ppermute only.
A program may use at most 64 MiB of HBM per device.

```python
import math
import jax
import jax.numpy as jnp
from jax import lax

CH = 1024
SHORT = 3
TOKENS = 8192


def draw_filters(key, part):
    key = jax.random.fold_in(key, 11)
    rate_key, noise_key = jax.random.split(key)
    positions = jnp.arange(TOKENS, dtype=jnp.float32)[:, None]
    log_rate = jax.random.uniform(rate_key, (CH,), jnp.float32, math.log(0.25 / TOKENS), math.log(1.0 / 32.0))
    noise_part = jax.random.truncated_normal(noise_key, -4.0, 4.0, (TOKENS, CH), jnp.float32)
    decay_rate = jnp.exp(log_rate)
    norm_scale = jnp.sqrt(jnp.expm1(-2.0 * decay_rate) / jnp.expm1(-2.0 * decay_rate * TOKENS))
    return noise_part * jnp.exp(-decay_rate[None, :] * positions) * norm_scale[None, :]


def level_of(rng, dims, pieces, low, top_value):
    factor_of, own = 1.0, jax.random.fold_in(rng, 6)
    for position, shards_of in pieces:
        steps = jnp.exp(jax.random.uniform(jax.random.fold_in(own, position), (shards_of,), jnp.float32, low / len(pieces), top_value / len(pieces)))
        factor_of = factor_of * jnp.repeat(steps, dims[position] // shards_of).reshape([-1 if axis == position else 1 for axis in range(len(dims))])
    return factor_of


def normal_values(rng, shape, scale, reach, cuts=(), held_as=jnp.bfloat16):
    drawn = jax.random.normal(rng, shape, jnp.float32) * scale
    if len(cuts) > 0:
        drawn = level_of(rng, shape, cuts, -0.22, 0.18) * drawn
    return jnp.clip(drawn, min=-reach, max=reach).astype(held_as)


def setup_inputs(seed: int = 0) -> dict:
    seeds = jax.random.split(jax.random.key(seed), 6)
    return {
        "projected": normal_values(seeds[0], (TOKENS, 3, CH), 1.0, 6.0, ((0, 32), (2, 4))),
        "short_taps": normal_values(seeds[1], (SHORT, 3, CH), SHORT ** -0.5, 3.5, ((2, 4),), jnp.float32),
        "filters": draw_filters(jax.random.fold_in(seeds[5], 71), 0),
        "skip_gain": normal_values(seeds[3], (CH,), 1.0, 4.0, ((0, 4),), jnp.float32),
        "out_weight": normal_values(seeds[4], (CH, CH), CH ** -0.5, 0.1875, ((0, 4),)),
    }


def reference(projected, short_taps, filters, skip_gain, out_weight):
    length = projected.shape[0]
    tap_count = short_taps.shape[0]
    widened = projected.astype(jnp.float32)
    padded = jnp.concatenate([jnp.zeros((tap_count - 1, 3, CH), jnp.float32), widened], axis=0)
    shaped = jnp.zeros((length, 3, CH), jnp.float32)
    for tap_index in range(tap_count):
        begin = tap_count - 1 - tap_index
        shaped = shaped + short_taps[tap_index] * padded[begin:begin + length]
    query_rows = shaped[:, 0, :]
    signal = (shaped[:, 1, :] * shaped[:, 2, :]).astype(jnp.bfloat16)
    signal_wide = lax.optimization_barrier(signal).astype(jnp.float32)
    blocks = CH // 128
    sig_blocks = signal_wide.reshape(length, blocks, 128).transpose(1, 0, 2)
    fil_blocks = filters.reshape(length, blocks, 128).transpose(1, 0, 2)

    def convolve(operands):
        sig_block, fil_block = operands
        spectrum = jnp.fft.rfft(sig_block, n=2 * length, axis=0) * jnp.fft.rfft(fil_block, n=2 * length, axis=0)
        return jnp.fft.irfft(spectrum, n=2 * length, axis=0)[:length].astype(jnp.float32)

    conv = lax.map(convolve, (sig_blocks, fil_blocks)).transpose(1, 0, 2).reshape(length, CH)
    gated = (query_rows * (conv + skip_gain * signal_wide)).astype(jnp.bfloat16)
    return jnp.dot(gated, out_weight, preferred_element_type=jnp.float32).astype(jnp.bfloat16)
```

```python
import math

import jax
import jax.numpy as jnp
import numpy as np
from jax import lax
from jax.experimental import pallas as pl
from jax.experimental.pallas import tpu as pltpu
from jax.sharding import PartitionSpec as P

BLOCKS = 32
SPAN = 256
OWN = 8
BF = jnp.bfloat16
F32 = jnp.float32


def dot(left, right):
    return jnp.dot(left, right, preferred_element_type=F32)


def constants():
    total = BLOCKS * SPAN
    low = np.arange(BLOCKS)[:, None] + 0.25
    coarse = 2 * math.pi / BLOCKS * low * np.arange(BLOCKS)[None, :]
    eye = np.eye(OWN)
    ahead = np.concatenate([np.kron(np.cos(coarse), eye), np.kron(-np.sin(coarse), eye)], axis=0)
    back = ahead.T / total
    turn = 2 * math.pi / total * low * np.arange(SPAN)[None, :]
    turn = np.repeat(turn, OWN, axis=0)
    fine = 2 * math.pi / SPAN * (np.arange(SPAN)[:, None] * np.arange(SPAN)[None, :] % SPAN)
    cos, sin = np.cos(fine), np.sin(fine)
    spread = np.block([[cos, -sin], [sin, cos]])
    gather = np.block([[cos, sin], [-sin, cos]])
    pick = np.zeros((SPAN, SPAN))
    order = np.zeros((SPAN, SPAN))
    for i in range(BLOCKS):
        for h in range(2):
            for c in range(4):
                pick[8 * i + 4 * h + c, 128 * h + 4 * i + c] = 1
                order[128 * h + 4 * i + c, 8 * i + 4 * h + c] = 1
    as_bf = lambda table: jnp.asarray(table.astype(np.float32)).astype(BF)
    as_f32 = lambda table: jnp.asarray(table.astype(np.float32))
    return dict(
        ahead=as_bf(ahead),
        back=as_bf(back),
        spread=as_bf(spread),
        gather=as_bf(gather),
        cos=as_f32(np.cos(turn)),
        sin=as_f32(np.sin(turn)),
        pick=as_bf(pick),
        order=as_bf(order),
    )


def pack_kernel(projected_ref, filters_ref, pick_ref, out_ref):
    pick = pick_ref[...]
    for which in range(4):
        rows = projected_ref[which] if which < 3 else filters_ref[...].astype(BF)
        turned = lax.dot_general(pick, rows, (((1,), (1,)), ((), ())), preferred_element_type=F32)
        first = turned[:, :128].reshape(BLOCKS, OWN, 128)
        second = turned[:, 128:].reshape(BLOCKS, OWN, 128)
        out_ref[:, 16 * which : 16 * which + 16, :] = jnp.concatenate([first, second], axis=1).astype(BF)


def conv_kernel(
    got_ref, taps_ref, skip_ref, ahead_ref, back_ref, spread_ref, gather_ref, cos_ref, sin_ref, order_ref, out_ref
):
    place = lax.axis_index("seq")
    lane = lax.broadcasted_iota(jnp.int32, (OWN, SPAN), 1)
    row = lax.broadcasted_iota(jnp.int32, (OWN, SPAN), 0)
    mine = lane == 128 * (row // 4) + 4 * place + row % 4

    def own(values):
        return jnp.sum(jnp.where(mine, values, 0.0), axis=1, keepdims=True)[None]

    def block(which):
        both = got_ref[:, 16 * which : 16 * which + 16, :].astype(F32)
        first = both[:, :8].reshape(SPAN, 128)
        second = both[:, 8:].reshape(SPAN, 128)
        return jnp.concatenate([first, second], axis=1)

    wide_lane = lax.broadcasted_iota(jnp.int32, (SPAN, SPAN), 1)

    def later(rows, by):
        turned = pltpu.roll(rows, by, 1)
        earlier = jnp.concatenate([jnp.zeros((OWN, SPAN), F32), turned[:-OWN]], axis=0)
        return jnp.where(wide_lane < by, earlier, turned)

    def shaped(which):
        rows = block(which)
        total = None
        for tap, moved in enumerate((rows, later(rows, 1), later(rows, 2))):
            gain = own(taps_ref[3 * tap + which : 3 * tap + which + 1, :])
            term = moved.reshape(BLOCKS, OWN, SPAN) * gain
            total = term if total is None else total + term
        return total.reshape(SPAN, SPAN)

    signal = (shaped(1) * shaped(2)).astype(BF)
    response = block(3).astype(BF)
    cos, sin = cos_ref[...], sin_ref[...]

    def spectrum(rows):
        real, imag = dot(ahead_ref[:SPAN], rows), dot(ahead_ref[SPAN:], rows)
        turned = jnp.concatenate([real * cos + imag * sin, imag * cos - real * sin], axis=1)
        both = dot(turned.astype(BF), spread_ref[...])
        return both[:, :SPAN], both[:, SPAN:]

    sig_real, sig_imag = spectrum(signal)
    res_real, res_imag = spectrum(response)
    product = jnp.concatenate(
        [sig_real * res_real - sig_imag * res_imag, sig_real * res_imag + sig_imag * res_real], axis=1
    )
    both = dot(product.astype(BF), gather_ref[...])
    real, imag = both[:, :SPAN], both[:, SPAN:]
    turned = jnp.concatenate([real * cos - imag * sin, real * sin + imag * cos], axis=0)
    conv = dot(back_ref[...], turned.astype(BF))
    skip = own(skip_ref[...])
    direct = (signal.astype(F32).reshape(BLOCKS, OWN, SPAN) * skip).reshape(SPAN, SPAN)
    gated = (shaped(0) * (conv + direct)).astype(BF)
    gated = dot(order_ref[...], gated)
    half = lax.broadcasted_iota(jnp.int32, (128, 128), 1) < 64
    for h in range(2):
        low = gated[:128, 128 * h : 128 * h + 128]
        high = gated[128:, 128 * h : 128 * h + 128]
        even = jnp.where(half, low, pltpu.roll(high, 64, 1))
        odd = jnp.where(half, pltpu.roll(low, 64, 1), high)
        out_ref[256 * h : 256 * h + 128, :] = even.astype(BF)
        out_ref[256 * h + 128 : 256 * h + 256, :] = odd.astype(BF)


def project_kernel(got_ref, w0_ref, w1_ref, w2_ref, w3_ref, out_ref):
    place = lax.axis_index("chan")
    total = None
    for step, weight_ref in enumerate((w0_ref, w1_ref, w2_ref, w3_ref)):
        owner = lax.rem(place + step, 4)
        rows = got_ref[pl.ds(pl.multiple_of(owner * 128, 128), 128), :].astype(F32).T
        gated = jnp.concatenate([rows[:64], rows[64:]], axis=1).astype(BF)
        term = dot(gated, weight_ref[...])
        total = term if total is None else total + term
    out_ref[...] = total.astype(BF)


def call(kernel, shape, *args, flops=0):
    return pl.pallas_call(
        kernel,
        out_shape=jax.ShapeDtypeStruct(shape, BF),
        compiler_params=pltpu.CompilerParams(vmem_limit_bytes=40 * 1024 * 1024),
    )(*args)


def on_device(projected, short_taps, filters, skip_gain, out_weight):
    table = constants()
    weights = [out_weight]
    for step in range(1, 4):
        weights.append(lax.ppermute(out_weight, "chan", [(i, (i - step) % 4) for i in range(4)]))
    packed = call(pack_kernel, (BLOCKS, 64, 128), projected.transpose(1, 0, 2), filters, table["pick"])
    got = lax.all_to_all(packed, "seq", split_axis=0, concat_axis=0, tiled=True)
    gated = call(
        conv_kernel,
        (512, 128),
        got,
        short_taps.reshape(9, SPAN),
        skip_gain.reshape(1, SPAN),
        *(table[name] for name in ("ahead", "back", "spread", "gather", "cos", "sin", "order")),
    )
    got = lax.all_to_all(gated.reshape(128, 4, 128), ("chan", "seq"), split_axis=0, concat_axis=0, tiled=True)
    return call(project_kernel, (64, 1024), got.reshape(512, 128), *weights)


def solution(mesh):
    return jax.shard_map(
        on_device,
        mesh=mesh,
        in_specs=(
            P("seq", None, "chan"),
            P(None, None, "chan"),
            P("seq", "chan"),
            P("chan"),
            P("chan", None),
        ),
        out_specs=P(("seq", "chan"), None),
        check_vma=False,
    )
```

```python
import math

import jax
import jax.numpy as jnp
import numpy as np
from jax import lax
from jax.experimental import pallas as pl
from jax.experimental.pallas import tpu as pltpu
from jax.sharding import PartitionSpec as P

BLOCKS = 32
SPAN = 256
OWN = 8
BF = jnp.bfloat16
F32 = jnp.float32


def dot(left, right):
    return jnp.dot(left, right, preferred_element_type=F32)


def constants():
    total = BLOCKS * SPAN
    low = np.arange(BLOCKS)[:, None] + 0.25
    coarse = 2 * math.pi / BLOCKS * low * np.arange(BLOCKS)[None, :]
    eye = np.eye(OWN)
    ahead = np.concatenate([np.kron(np.cos(coarse), eye), np.kron(-np.sin(coarse), eye)], axis=0)
    back = ahead.T / total
    turn = 2 * math.pi / total * low * np.arange(SPAN)[None, :]
    turn = np.repeat(turn, OWN, axis=0)
    fine = 2 * math.pi / SPAN * (np.arange(SPAN)[:, None] * np.arange(SPAN)[None, :] % SPAN)
    as_bf = lambda table: jnp.asarray(table.astype(np.float32)).astype(BF)
    return dict(
        ahead=as_bf(ahead),
        back=as_bf(back),
        fine=as_bf(np.concatenate([np.cos(fine), np.sin(fine)], axis=0)),
        turn=as_bf(np.concatenate([np.cos(turn), np.sin(turn)], axis=0)),
    )


def message_order(transposed):
    row = lax.broadcasted_iota(jnp.int32, (SPAN, SPAN), 0)
    column = lax.broadcasted_iota(jnp.int32, (SPAN, SPAN), 1)
    if transposed:
        row, column = column, row
    place = 128 * ((row >> 2) & 1) + 4 * (row >> 3) + (row & 3)
    return jnp.where(place == column, 1.0, 0.0).astype(BF)


def pack_kernel(projected_ref, filters_ref, out_ref, rows_ref, taps_ref, sent_ref, in_sems, out_sems):
    reads = []
    for which in (3, 0, 1, 2):
        source = projected_ref.at[which] if which < 3 else filters_ref
        target = rows_ref.at[which] if which < 3 else taps_ref
        reads.append((which, pltpu.make_async_copy(source, target, in_sems.at[which])))
    for _, read in reads:
        read.start()
    pick = message_order(False)
    writes = []
    for which, read in reads:
        read.wait()
        rows = rows_ref[which] if which < 3 else taps_ref[...].astype(BF)
        turned = lax.dot_general(pick, rows, (((1,), (1,)), ((), ())), preferred_element_type=F32)
        first = turned[:, :128].reshape(BLOCKS, OWN, 128)
        second = turned[:, 128:].reshape(BLOCKS, OWN, 128)
        sent_ref[which] = jnp.concatenate([first, second], axis=1).astype(BF)
        write = pltpu.make_async_copy(
            sent_ref.at[which], out_ref.at[:, pl.ds(16 * which, 16), :], out_sems.at[which]
        )
        write.start()
        writes.append(write)
    for write in writes:
        write.wait()


def conv_kernel(got_ref, taps_hbm, skip_hbm, ahead_hbm, fine_hbm, turn_hbm, back_hbm, out_ref, *scratch):
    taps_ref, skip_ref, ahead_ref, fine_ref, turn_ref, back_ref, sems = scratch
    reads = []
    for n, (source, target) in enumerate(
        zip((ahead_hbm, taps_hbm, turn_hbm, fine_hbm, skip_hbm, back_hbm),
            (ahead_ref, taps_ref, turn_ref, fine_ref, skip_ref, back_ref))
    ):
        reads.append(pltpu.make_async_copy(source, target, sems.at[n]))
        reads[-1].start()
    ahead_read, taps_read, turn_read, fine_read, skip_read, back_read = reads

    place = lax.axis_index("seq")
    lane = lax.broadcasted_iota(jnp.int32, (OWN, SPAN), 1)
    row = lax.broadcasted_iota(jnp.int32, (OWN, SPAN), 0)
    mine = lane == 128 * (row >> 2) + 4 * place + (row & 3)

    def own(values):
        return jnp.sum(jnp.where(mine, values, 0.0), axis=1, keepdims=True)[None]

    def block(which):
        both = got_ref[:, 16 * which : 16 * which + 16, :].astype(F32)
        first = both[:, :8].reshape(SPAN, 128)
        second = both[:, 8:].reshape(SPAN, 128)
        return jnp.concatenate([first, second], axis=1)

    wide_lane = lax.broadcasted_iota(jnp.int32, (SPAN, SPAN), 1)

    def later(rows, by):
        turned = pltpu.roll(rows, by, 1)
        earlier = jnp.concatenate([jnp.zeros((OWN, SPAN), F32), turned[:-OWN]], axis=0)
        return jnp.where(wide_lane < by, earlier, turned)

    def shaped(which):
        rows = block(which)
        total = None
        for tap, moved in enumerate((rows, later(rows, 1), later(rows, 2))):
            gain = own(taps_ref[tap, which : which + 1, :])
            term = moved.reshape(BLOCKS, OWN, SPAN) * gain
            total = term if total is None else total + term
        return total.reshape(SPAN, SPAN)

    response = block(3).astype(BF)
    taps_read.wait()
    signal = (shaped(1) * shaped(2)).astype(BF)
    ahead_read.wait()
    res_half = dot(ahead_ref[...], response)
    sig_half = dot(ahead_ref[...], signal)
    turn_read.wait()
    cos, sin = turn_ref[:SPAN].astype(F32), turn_ref[SPAN:].astype(F32)
    fine_read.wait()
    fine_cos, fine_sin = fine_ref[:SPAN], fine_ref[SPAN:]
    fine_less = -fine_sin
    spread = jnp.concatenate(
        [jnp.concatenate([fine_cos, fine_less], axis=1), jnp.concatenate([fine_sin, fine_cos], axis=1)], axis=0
    )
    gather = jnp.concatenate(
        [jnp.concatenate([fine_cos, fine_sin], axis=1), jnp.concatenate([fine_less, fine_cos], axis=1)], axis=0
    )

    def spectrum(half):
        real, imag = half[:SPAN], half[SPAN:]
        turned = jnp.concatenate([real * cos + imag * sin, imag * cos - real * sin], axis=1)
        both = dot(turned.astype(BF), spread)
        return both[:, :SPAN], both[:, SPAN:]

    res_real, res_imag = spectrum(res_half)
    sig_real, sig_imag = spectrum(sig_half)
    product = jnp.concatenate(
        [sig_real * res_real - sig_imag * res_imag, sig_real * res_imag + sig_imag * res_real], axis=1
    )
    both = dot(product.astype(BF), gather)
    real, imag = both[:, :SPAN], both[:, SPAN:]
    turned = jnp.concatenate([real * cos - imag * sin, real * sin + imag * cos], axis=0)
    skip_read.wait()
    back_read.wait()
    conv = dot(back_ref[...], turned.astype(BF))
    skip = own(skip_ref[...])
    direct = (signal.astype(F32).reshape(BLOCKS, OWN, SPAN) * skip).reshape(SPAN, SPAN)
    gated = (shaped(0) * (conv + direct)).astype(BF)
    gated = dot(message_order(True), gated)
    half = lax.broadcasted_iota(jnp.int32, (128, 128), 1) < 64
    for h in range(2):
        low = gated[:128, 128 * h : 128 * h + 128]
        high = gated[128:, 128 * h : 128 * h + 128]
        even = jnp.where(half, low, pltpu.roll(high, 64, 1))
        odd = jnp.where(half, pltpu.roll(low, 64, 1), high)
        out_ref[256 * h : 256 * h + 128, :] = even.astype(BF)
        out_ref[256 * h + 128 : 256 * h + 256, :] = odd.astype(BF)


def project_kernel(got_ref, own_ref, near_ref, swap_ref, far_ref, far_swap_ref, out_ref):
    place = lax.axis_index("chan")
    odd = lax.axis_index("seq") % 2

    def halves(step):
        owner = lax.rem(place + step, 4)
        rows = got_ref[pl.ds(pl.multiple_of(owner * 128, 128), 128), :].astype(F32).T
        return rows[:64], rows[64:]

    total = None
    for step, weight_ref in ((0, own_ref), (1 + 2 * odd, near_ref), (3 - 2 * odd, swap_ref)):
        term = dot(jnp.concatenate(halves(step), axis=1).astype(BF), weight_ref[...])
        total = term if total is None else total + term
    low, high = halves(2)
    total = total + dot(jnp.where(odd == 0, low, high).astype(BF), far_ref[...])
    total = total + dot(jnp.where(odd == 0, high, low).astype(BF), far_swap_ref[...])
    out_ref[...] = total.astype(BF)


HBM = pl.BlockSpec(memory_space=pltpu.HBM)
VMEM = pl.BlockSpec(memory_space=pltpu.VMEM)
PARAMS = pltpu.CompilerParams(vmem_limit_bytes=32 * 1024 * 1024)


TINY = pl.CostEstimate(flops=1000, bytes_accessed=1000, transcendentals=0)


def pack(projected, filters):
    return pl.pallas_call(
        pack_kernel,
        out_shape=jax.ShapeDtypeStruct((BLOCKS, 64, 128), BF),
        in_specs=[HBM, HBM],
        out_specs=HBM,
        scratch_shapes=[
            pltpu.VMEM((3, SPAN, SPAN), BF),
            pltpu.VMEM((SPAN, SPAN), F32),
            pltpu.VMEM((4, BLOCKS, 16, 128), BF),
            pltpu.SemaphoreType.DMA((4,)),
            pltpu.SemaphoreType.DMA((4,)),
        ],
        cost_estimate=TINY,
    )(projected.transpose(1, 0, 2), filters)


def convolve(got, short_taps, skip_gain):
    table = constants()
    held = [short_taps, skip_gain.reshape(1, SPAN)] + [table[name] for name in ("ahead", "fine", "turn", "back")]
    return pl.pallas_call(
        conv_kernel,
        out_shape=jax.ShapeDtypeStruct((512, 128), BF),
        in_specs=[VMEM] + [HBM] * 6,
        out_specs=VMEM,
        scratch_shapes=[pltpu.VMEM(array.shape, array.dtype) for array in held] + [pltpu.SemaphoreType.DMA((6,))],
        compiler_params=PARAMS,
        cost_estimate=TINY,
    )(got, *held)


def project(got, weights):
    return pl.pallas_call(
        project_kernel,
        out_shape=jax.ShapeDtypeStruct((64, 1024), BF),
        in_specs=[VMEM] * (1 + len(weights)),
        out_specs=VMEM,
        compiler_params=PARAMS,
        cost_estimate=TINY,
    )(got, *weights)


def on_device(projected, short_taps, filters, skip_gain, out_weight):
    near = lax.ppermute(
        out_weight,
        ("seq", "chan"),
        [(s * 4 + (j + (1 if s % 2 == 0 else 3)) % 4, s * 4 + j) for s in range(BLOCKS) for j in range(4)],
    )
    half = lax.dynamic_slice_in_dim(out_weight, 128 * (lax.axis_index("seq") % 2), 128, 0)
    far = lax.ppermute(half, "chan", [(j, (j + 2) % 4) for j in range(4)])
    got = lax.all_to_all(pack(projected, filters), "seq", split_axis=0, concat_axis=0, tiled=True)
    gated = convolve(got, short_taps, skip_gain)
    gated, near, far = lax.optimization_barrier((gated, near, far))
    pairs = [(s, s ^ 1) for s in range(BLOCKS)]
    weights = (out_weight, near, lax.ppermute(near, "seq", pairs), far, lax.ppermute(far, "seq", pairs))
    got = lax.all_to_all(gated.reshape(128, 4, 128), ("chan", "seq"), split_axis=0, concat_axis=0, tiled=True)
    return project(got.reshape(512, 128), weights)


def solution(mesh):
    return jax.shard_map(
        on_device,
        mesh=mesh,
        in_specs=(
            P("seq", None, "chan"),
            P(None, None, "chan"),
            P("seq", "chan"),
            P("chan"),
            P("chan", None),
        ),
        out_specs=P(("seq", "chan"), None),
        check_vma=False,
    )
```

```python
import math

import jax
import jax.numpy as jnp
import numpy as np
from jax import lax
from jax.experimental import pallas as pl
from jax.experimental.pallas import tpu as pltpu
from jax.sharding import PartitionSpec as P

BLOCKS = 32
SPAN = 256
OWN = 8
BF = jnp.bfloat16
F32 = jnp.float32


def dot(left, right):
    return jnp.dot(left, right, preferred_element_type=F32)


def constants():
    total = BLOCKS * SPAN
    low = np.arange(BLOCKS)[:, None] + 0.25
    coarse = 2 * math.pi / BLOCKS * low * np.arange(BLOCKS)[None, :]
    eye = np.eye(OWN)
    ahead = np.concatenate([np.kron(np.cos(coarse), eye), np.kron(-np.sin(coarse), eye)], axis=0)
    back = ahead.T / total
    turn = 2 * math.pi / total * low * np.arange(SPAN)[None, :]
    turn = np.repeat(turn, OWN, axis=0)
    fine = 2 * math.pi / SPAN * (np.arange(SPAN)[:, None] * np.arange(SPAN)[None, :] % SPAN)
    as_bf = lambda table: jnp.asarray(table.astype(np.float32)).astype(BF)
    return dict(
        ahead=as_bf(ahead),
        back=as_bf(back),
        fine=as_bf(np.concatenate([np.cos(fine), np.sin(fine)], axis=0)),
        turn=as_bf(np.concatenate([np.cos(turn), np.sin(turn)], axis=0)),
    )


def swap_halves(tiles):
    count, _, columns = tiles.shape
    pairs = tiles.reshape(count // 2, 2, 8, columns)
    first, second = pairs[:, 0], pairs[:, 1]
    upper = lax.broadcasted_iota(jnp.int32, first.shape, 1) < 4
    return (
        jnp.where(upper, first, pltpu.roll(second, 4, 1)),
        jnp.where(upper, pltpu.roll(first, 4, 1), second),
    )


def pack_kernel(projected_ref, filters_ref, out_ref, rows_ref, taps_ref, sent_ref, in_sems, out_sems):
    reads = []
    for which in (3, 0, 1, 2):
        source = projected_ref.at[which] if which < 3 else filters_ref
        target = rows_ref.at[which] if which < 3 else taps_ref
        reads.append((which, pltpu.make_async_copy(source, target, in_sems.at[which])))
    for _, read in reads:
        read.start()
    writes = []
    for which, read in reads:
        read.wait()
        rows = rows_ref[which] if which < 3 else taps_ref[...].astype(BF)
        turned = rows.T.astype(F32).reshape(2, BLOCKS // 2, OWN, SPAN)
        both = jnp.stack([turned[0], turned[1]], axis=1).reshape(BLOCKS, OWN, SPAN)
        both = jnp.stack(swap_halves(both), axis=1).reshape(BLOCKS, OWN, SPAN)
        sent_ref[which] = jnp.concatenate([both[:, :, :128], both[:, :, 128:]], axis=1).astype(BF)
        write = pltpu.make_async_copy(
            sent_ref.at[which], out_ref.at[:, pl.ds(16 * which, 16), :], out_sems.at[which]
        )
        write.start()
        writes.append(write)
    for write in writes:
        write.wait()


def conv_kernel(got_ref, taps_ref, skip_ref, ahead_ref, fine_ref, turn_ref, back_ref, out_ref):
    place = lax.axis_index("seq")
    lane = lax.broadcasted_iota(jnp.int32, (OWN, SPAN), 1)
    row = lax.broadcasted_iota(jnp.int32, (OWN, SPAN), 0)
    mine = lane == 128 * (row >> 2) + 4 * place + (row & 3)

    def own(values):
        return jnp.sum(jnp.where(mine, values, 0.0), axis=1, keepdims=True)[None]

    def block(which):
        both = got_ref[:, 16 * which : 16 * which + 16, :].astype(F32)
        first = both[:, :8].reshape(SPAN, 128)
        second = both[:, 8:].reshape(SPAN, 128)
        return jnp.concatenate([first, second], axis=1)

    wide_lane = lax.broadcasted_iota(jnp.int32, (SPAN, SPAN), 1)

    def later(rows, by):
        turned = pltpu.roll(rows, by, 1)
        earlier = jnp.concatenate([jnp.zeros((OWN, SPAN), F32), turned[:-OWN]], axis=0)
        return jnp.where(wide_lane < by, earlier, turned)

    def shaped(which):
        rows = block(which)
        total = None
        for tap, moved in enumerate((rows, later(rows, 1), later(rows, 2))):
            gain = own(taps_ref[tap, which : which + 1, :])
            term = moved.reshape(BLOCKS, OWN, SPAN) * gain
            total = term if total is None else total + term
        return total.reshape(SPAN, SPAN)

    response = block(3).astype(BF)
    signal = (shaped(1) * shaped(2)).astype(BF)
    res_half = dot(ahead_ref[...], response)
    sig_half = dot(ahead_ref[...], signal)
    cos, sin = turn_ref[:SPAN].astype(F32), turn_ref[SPAN:].astype(F32)
    fine_cos, fine_sin = fine_ref[:SPAN], fine_ref[SPAN:]
    fine_less = -fine_sin
    spread = jnp.concatenate(
        [jnp.concatenate([fine_cos, fine_less], axis=1), jnp.concatenate([fine_sin, fine_cos], axis=1)], axis=0
    )
    gather = jnp.concatenate(
        [jnp.concatenate([fine_cos, fine_sin], axis=1), jnp.concatenate([fine_less, fine_cos], axis=1)], axis=0
    )

    def spectrum(half):
        real, imag = half[:SPAN], half[SPAN:]
        turned = jnp.concatenate([real * cos + imag * sin, imag * cos - real * sin], axis=1)
        both = dot(turned.astype(BF), spread)
        return both[:, :SPAN], both[:, SPAN:]

    res_real, res_imag = spectrum(res_half)
    sig_real, sig_imag = spectrum(sig_half)
    product = jnp.concatenate(
        [sig_real * res_real - sig_imag * res_imag, sig_real * res_imag + sig_imag * res_real], axis=1
    )
    both = dot(product.astype(BF), gather)
    real, imag = both[:, :SPAN], both[:, SPAN:]
    turned = jnp.concatenate([real * cos - imag * sin, real * sin + imag * cos], axis=0)
    conv = dot(back_ref[...], turned.astype(BF))
    skip = own(skip_ref[...])
    direct = (signal.astype(F32).reshape(BLOCKS, OWN, SPAN) * skip).reshape(SPAN, SPAN)
    gated = shaped(0) * (conv + direct)
    lows, highs = (rows.reshape(128, SPAN) for rows in swap_halves(gated.reshape(BLOCKS, OWN, SPAN)))
    half = lax.broadcasted_iota(jnp.int32, (128, 128), 1) < 64
    for h in range(2):
        low = lows[:, 128 * h : 128 * h + 128]
        high = highs[:, 128 * h : 128 * h + 128]
        even = jnp.where(half, low, pltpu.roll(high, 64, 1))
        odd = jnp.where(half, pltpu.roll(low, 64, 1), high)
        out_ref[256 * h : 256 * h + 128, :] = even.astype(BF)
        out_ref[256 * h + 128 : 256 * h + 256, :] = odd.astype(BF)


def project_kernel(got_ref, own_ref, near_ref, swap_ref, far_ref, far_swap_ref, out_ref):
    place = lax.axis_index("chan")
    odd = lax.axis_index("seq") % 2

    def halves(step):
        owner = lax.rem(place + step, 4)
        rows = got_ref[pl.ds(pl.multiple_of(owner * 128, 128), 128), :].astype(F32).T
        return rows[:64], rows[64:]

    total = None
    for step, weight_ref in ((0, own_ref), (1 + 2 * odd, near_ref), (3 - 2 * odd, swap_ref)):
        term = dot(jnp.concatenate(halves(step), axis=1).astype(BF), weight_ref[...])
        total = term if total is None else total + term
    low, high = halves(2)
    total = total + dot(jnp.where(odd == 0, low, high).astype(BF), far_ref[...])
    total = total + dot(jnp.where(odd == 0, high, low).astype(BF), far_swap_ref[...])
    out_ref[...] = total.astype(BF)


HBM = pl.BlockSpec(memory_space=pltpu.HBM)
VMEM = pl.BlockSpec(memory_space=pltpu.VMEM)
PARAMS = pltpu.CompilerParams(vmem_limit_bytes=32 * 1024 * 1024)


TINY = pl.CostEstimate(flops=1000, bytes_accessed=1000, transcendentals=0)


def pack(projected, filters):
    return pl.pallas_call(
        pack_kernel,
        out_shape=jax.ShapeDtypeStruct((BLOCKS, 64, 128), BF),
        in_specs=[HBM, HBM],
        out_specs=HBM,
        scratch_shapes=[
            pltpu.VMEM((3, SPAN, SPAN), BF),
            pltpu.VMEM((SPAN, SPAN), F32),
            pltpu.VMEM((4, BLOCKS, 16, 128), BF),
            pltpu.SemaphoreType.DMA((4,)),
            pltpu.SemaphoreType.DMA((4,)),
        ],
        cost_estimate=TINY,
    )(projected.transpose(1, 0, 2), filters)


def convolve(got, short_taps, skip_gain):
    table = constants()
    held = [short_taps, skip_gain.reshape(1, SPAN)] + [table[name] for name in ("ahead", "fine", "turn", "back")]
    return pl.pallas_call(
        conv_kernel,
        out_shape=jax.ShapeDtypeStruct((512, 128), BF),
        in_specs=[VMEM] * 7,
        out_specs=VMEM,
        compiler_params=PARAMS,
        cost_estimate=TINY,
    )(got, *held)


def project(got, weights):
    return pl.pallas_call(
        project_kernel,
        out_shape=jax.ShapeDtypeStruct((64, 1024), BF),
        in_specs=[VMEM] * (1 + len(weights)),
        out_specs=VMEM,
        compiler_params=PARAMS,
        cost_estimate=TINY,
    )(got, *weights)


def on_device(projected, short_taps, filters, skip_gain, out_weight):
    ring = [(s * 4 + (j + (1 if s % 2 == 0 else 3)) % 4, s * 4 + j) for s in range(BLOCKS) for j in range(4)]
    near = lax.ppermute(out_weight, ("seq", "chan"), ring)
    half = lax.dynamic_slice_in_dim(near, 128 * (lax.axis_index("seq") & 1), 128, 0)
    far = lax.ppermute(half, ("seq", "chan"), ring)
    got = lax.all_to_all(pack(projected, filters), "seq", split_axis=0, concat_axis=0, tiled=True)
    gated = convolve(got, short_taps, skip_gain)
    gated, near, far = lax.optimization_barrier((gated, near, far))
    pairs = [(s, s ^ 1) for s in range(BLOCKS)]
    weights = (out_weight, near, lax.ppermute(near, "seq", pairs), far, lax.ppermute(far, "seq", pairs))
    got = lax.all_to_all(gated.reshape(128, 4, 128), ("chan", "seq"), split_axis=0, concat_axis=0, tiled=True)
    return project(got.reshape(512, 128), weights)


def solution(mesh):
    return jax.shard_map(
        on_device,
        mesh=mesh,
        in_specs=(
            P("seq", None, "chan"),
            P(None, None, "chan"),
            P("seq", "chan"),
            P("chan"),
            P("chan", None),
        ),
        out_specs=P(("seq", "chan"), None),
        check_vma=False,
    )
```

```python
import math

import jax
import jax.numpy as jnp
import numpy as np
from jax import lax
from jax.experimental import pallas as pl
from jax.experimental.pallas import tpu as pltpu
from jax.sharding import PartitionSpec as P

BLOCKS = 32
SPAN = 256
OWN = 8
BF = jnp.bfloat16
F32 = jnp.float32


def dot(left, right):
    return jnp.dot(left, right, preferred_element_type=F32)


def constants():
    total = BLOCKS * SPAN
    low = np.arange(BLOCKS)[:, None] + 0.25
    coarse = 2 * math.pi / BLOCKS * low * np.arange(BLOCKS)[None, :]
    eye = np.eye(OWN)
    ahead = np.concatenate([np.kron(np.cos(coarse), eye), np.kron(-np.sin(coarse), eye)], axis=0)
    back = ahead.T / total
    turn = 2 * math.pi / total * low * np.arange(SPAN)[None, :]
    turn = np.repeat(turn, OWN, axis=0)
    fine = 2 * math.pi / SPAN * (np.arange(SPAN)[:, None] * np.arange(SPAN)[None, :] % SPAN)
    as_bf = lambda table: jnp.asarray(table.astype(np.float32)).astype(BF)
    return dict(
        ahead=as_bf(ahead),
        back=as_bf(back),
        fine=as_bf(np.concatenate([np.cos(fine), np.sin(fine)], axis=0)),
        turn=as_bf(np.concatenate([np.cos(turn), np.sin(turn)], axis=0)),
    )


def swap_halves(tiles):
    count, _, columns = tiles.shape
    pairs = tiles.reshape(count // 2, 2, 8, columns)
    first, second = pairs[:, 0], pairs[:, 1]
    upper = lax.broadcasted_iota(jnp.int32, first.shape, 1) < 4
    return (
        jnp.where(upper, first, pltpu.roll(second, 4, 1)),
        jnp.where(upper, pltpu.roll(first, 4, 1), second),
    )


def pack_kernel(projected_ref, filters_ref, taps_hbm, out_ref, rows_ref, long_ref, taps_ref, sent_ref, sems):
    parts = (
        (filters_ref, long_ref),
        (taps_hbm, taps_ref),
        (projected_ref.at[0], rows_ref.at[0]),
        (projected_ref.at[1], rows_ref.at[1]),
        (projected_ref.at[2], rows_ref.at[2]),
    )
    reads = [pltpu.make_async_copy(*part, sems.at[n]) for n, part in enumerate(parts)]
    for read in reads:
        read.start()

    def by_device(turned):
        columns = turned.shape[1]
        turned = turned.astype(F32).reshape(2, BLOCKS // 2, OWN, columns)
        both = jnp.stack([turned[0], turned[1]], axis=1).reshape(BLOCKS, OWN, columns)
        return jnp.stack(swap_halves(both), axis=1).reshape(BLOCKS, OWN, columns)

    def store(first_row, rows):
        both = by_device(rows.T)
        sent_ref[:, first_row : first_row + 16, :] = jnp.concatenate([both[:, :, :128], both[:, :, 128:]], axis=1).astype(BF)

    reads[0].wait()
    store(16, long_ref[...].astype(BF))
    reads[2].wait()
    store(32, rows_ref[0])
    for read in (reads[1], reads[3], reads[4]):
        read.wait()

    def shaped(which):
        rows = rows_ref[which].astype(F32)
        total = taps_ref[0, which : which + 1, :] * rows
        for tap in (1, 2):
            total = total + taps_ref[tap, which : which + 1, :] * pltpu.roll(rows, tap, 0)
        return total

    store(0, (shaped(1) * shaped(2)).astype(BF))
    key, value = rows_ref[1], rows_ref[2]
    first = [rows[:16].astype(F32)[:2] for rows in (key, value)]
    last = [rows[SPAN - 16 :].astype(F32)[14:] for rows in (key, value)]
    edges = jnp.concatenate(first + last + [jnp.zeros((120, SPAN), F32)], axis=0)
    sent_ref[:, 48:56, :] = by_device(edges.T).astype(BF)
    write = pltpu.make_async_copy(sent_ref, out_ref, sems.at[5])
    write.start()
    write.wait()


def conv_kernel(got_ref, taps_ref, skip_ref, ahead_ref, fine_ref, turn_ref, back_ref, out_ref):
    place = lax.axis_index("seq")
    lane = lax.broadcasted_iota(jnp.int32, (OWN, SPAN), 1)
    row = lax.broadcasted_iota(jnp.int32, (OWN, SPAN), 0)
    mine = lane == 128 * (row >> 2) + 4 * place + (row & 3)

    def own(values):
        return jnp.sum(jnp.where(mine, values, 0.0), axis=1, keepdims=True)[None]

    def block(first_row):
        both = got_ref[:, first_row : first_row + 16, :].astype(F32)
        return both[:, :8], both[:, 8:]

    edges = got_ref[:, 48:56, :].astype(F32)
    before = jnp.concatenate([jnp.zeros((1, OWN, 128), F32), edges[:-1]], axis=0)
    thin = lax.broadcasted_iota(jnp.int32, (BLOCKS, OWN, 128), 2)

    def left(rows, by):
        return rows if by == 0 else pltpu.roll(rows, -by % 128, 2)

    def gains(which):
        return [own(taps_ref[tap, which : which + 1, :]) for tap in range(3)]

    def edge(which, at):
        first, second, third = gains(which)
        once = jnp.where(thin == 0, left(before, at + 5), left(edges, at - 1))
        return left(edges, at) * first + once * second + left(before, at + 4) * third

    def later(rows, by):
        turned = pltpu.roll(rows, by, 2)
        earlier = jnp.concatenate([jnp.zeros((1, OWN, SPAN), F32), turned[:-1]], axis=0)
        return jnp.where(lax.broadcasted_iota(jnp.int32, turned.shape, 2) < by, earlier, turned)

    early, late = block(0)
    early = jnp.where(thin < 2, edge(1, 0) * edge(2, 2), early)
    signal = jnp.concatenate([early.reshape(SPAN, 128), late.reshape(SPAN, 128)], axis=1).astype(BF)
    response = jnp.concatenate([half.reshape(SPAN, 128) for half in block(16)], axis=1).astype(BF)
    res_half = dot(ahead_ref[...], response)
    sig_half = dot(ahead_ref[...], signal)
    raw = jnp.concatenate(block(32), axis=2)
    first, second, third = gains(0)
    query = raw * first + later(raw, 1) * second + later(raw, 2) * third
    cos, sin = turn_ref[:SPAN].astype(F32), turn_ref[SPAN:].astype(F32)
    fine_cos, fine_sin = fine_ref[:SPAN], fine_ref[SPAN:]
    fine_less = -fine_sin
    spread = jnp.concatenate(
        [jnp.concatenate([fine_cos, fine_less], axis=1), jnp.concatenate([fine_sin, fine_cos], axis=1)], axis=0
    )
    gather = jnp.concatenate(
        [jnp.concatenate([fine_cos, fine_sin], axis=1), jnp.concatenate([fine_less, fine_cos], axis=1)], axis=0
    )

    def spectrum(half):
        real, imag = half[:SPAN], half[SPAN:]
        turned = jnp.concatenate([real * cos + imag * sin, imag * cos - real * sin], axis=1)
        both = dot(turned.astype(BF), spread)
        return both[:, :SPAN], both[:, SPAN:]

    res_real, res_imag = spectrum(res_half)
    sig_real, sig_imag = spectrum(sig_half)
    product = jnp.concatenate(
        [sig_real * res_real - sig_imag * res_imag, sig_real * res_imag + sig_imag * res_real], axis=1
    )
    both = dot(product.astype(BF), gather)
    real, imag = both[:, :SPAN], both[:, SPAN:]
    turned = jnp.concatenate([real * cos - imag * sin, real * sin + imag * cos], axis=0)
    conv = dot(back_ref[...], turned.astype(BF))
    skip = own(skip_ref[...])
    direct = (signal.astype(F32).reshape(BLOCKS, OWN, SPAN) * skip).reshape(SPAN, SPAN)
    gated = query * (conv + direct).reshape(BLOCKS, OWN, SPAN)
    lows, highs = (rows.reshape(128, SPAN) for rows in swap_halves(gated))
    half = lax.broadcasted_iota(jnp.int32, (128, 128), 1) < 64
    for h in range(2):
        low, high = lows[:, 128 * h : 128 * h + 128], highs[:, 128 * h : 128 * h + 128]
        even = jnp.where(half, low, pltpu.roll(high, 64, 1))
        odd = jnp.where(half, pltpu.roll(low, 64, 1), high)
        out_ref[256 * h : 256 * h + 128, :] = even.astype(BF)
        out_ref[256 * h + 128 : 256 * h + 256, :] = odd.astype(BF)


def project_kernel(got_ref, own_ref, near_ref, swap_ref, other_ref, far_ref, far_swap_ref, out_ref):
    place = lax.axis_index("chan")
    odd = lax.axis_index("seq") % 2

    def block(step):
        owner = lax.rem(place + step, 4)
        rows = got_ref[pl.ds(pl.multiple_of(owner * 128, 128), 128), :].astype(F32).T
        return jnp.concatenate([rows[:64], rows[64:]], axis=1).astype(BF)

    total = dot(block(0), own_ref[...]) + dot(block(1 + 2 * odd), near_ref[...])
    for step, here_ref, there_ref in ((3 - 2 * odd, other_ref, swap_ref), (2, far_ref, far_swap_ref)):
        rows = block(step)
        total = total + dot(jnp.where(odd == 0, rows[:, :128], rows[:, 128:]), here_ref[...])
        total = total + dot(jnp.where(odd == 0, rows[:, 128:], rows[:, :128]), there_ref[...])
    out_ref[...] = total.astype(BF)


HBM = pl.BlockSpec(memory_space=pltpu.HBM)
VMEM = pl.BlockSpec(memory_space=pltpu.VMEM)
PARAMS = pltpu.CompilerParams(vmem_limit_bytes=32 * 1024 * 1024)


TINY = pl.CostEstimate(flops=1000, bytes_accessed=1000, transcendentals=0)


def pack(projected, filters, short_taps):
    return pl.pallas_call(
        pack_kernel,
        out_shape=jax.ShapeDtypeStruct((BLOCKS, 56, 128), BF),
        in_specs=[HBM] * 3,
        out_specs=HBM,
        scratch_shapes=[
            pltpu.VMEM((3, SPAN, SPAN), BF),
            pltpu.VMEM((SPAN, SPAN), F32),
            pltpu.VMEM((3, 3, SPAN), F32),
            pltpu.VMEM((BLOCKS, 56, 128), BF),
            pltpu.SemaphoreType.DMA((6,)),
        ],
        cost_estimate=TINY,
    )(projected, filters, short_taps)


def convolve(got, short_taps, skip_gain):
    table = constants()
    held = [short_taps, skip_gain.reshape(1, SPAN)] + [table[name] for name in ("ahead", "fine", "turn", "back")]
    return pl.pallas_call(
        conv_kernel,
        out_shape=jax.ShapeDtypeStruct((512, 128), BF),
        in_specs=[VMEM] * 7,
        out_specs=VMEM,
        compiler_params=PARAMS,
        cost_estimate=TINY,
    )(got, *held)


def project(got, weights):
    return pl.pallas_call(
        project_kernel,
        out_shape=jax.ShapeDtypeStruct((64, 1024), BF),
        in_specs=[VMEM] * (1 + len(weights)),
        out_specs=VMEM,
        compiler_params=PARAMS,
        cost_estimate=TINY,
    )(got, *weights)


def on_device(projected, short_taps, filters, skip_gain, out_weight):
    ring = [(s * 4 + (j + (1 if s % 2 == 0 else 3)) % 4, s * 4 + j) for s in range(BLOCKS) for j in range(4)]
    near = lax.ppermute(out_weight, ("seq", "chan"), ring)
    core = lax.axis_index("seq") & 1
    half = lax.dynamic_slice_in_dim(near, 128 * core, 128, 0)
    other = lax.dynamic_slice_in_dim(near, 128 - 128 * core, 128, 0)
    far = lax.ppermute(half, ("seq", "chan"), ring)
    pairs = [(s, s ^ 1) for s in range(BLOCKS)]
    swaps = [lax.ppermute(part, "seq", pairs) for part in (half, other)]
    got = lax.all_to_all(pack(projected.transpose(1, 0, 2), filters, short_taps), "seq", split_axis=0, concat_axis=0, tiled=True)
    got, *swaps = lax.optimization_barrier((got, *swaps))
    gated = convolve(got, short_taps, skip_gain)
    gated, far = lax.optimization_barrier((gated, far))
    weights = (out_weight, near, *swaps, far, lax.ppermute(far, "seq", pairs))
    got = lax.all_to_all(gated.reshape(128, 4, 128), ("chan", "seq"), split_axis=0, concat_axis=0, tiled=True)
    return project(got.reshape(512, 128), weights)


def solution(mesh):
    return jax.shard_map(
        on_device,
        mesh=mesh,
        in_specs=(
            P("seq", None, "chan"),
            P(None, None, "chan"),
            P("seq", "chan"),
            P("chan"),
            P("chan", None),
        ),
        out_specs=P(("seq", "chan"), None),
        check_vma=False,
    )
```

```python
import math

import jax
import jax.numpy as jnp
import numpy as np
from jax import lax
from jax.experimental import pallas as pl
from jax.experimental.pallas import tpu as pltpu
from jax.sharding import PartitionSpec as P

BLOCKS = 32
SPAN = 256
OWN = 8
BF = jnp.bfloat16
F32 = jnp.float32


def dot(left, right):
    return jnp.dot(left, right, preferred_element_type=F32)


def constants():
    total = BLOCKS * SPAN
    low = np.arange(BLOCKS)[:, None] + 0.25
    coarse = 2 * math.pi / BLOCKS * low * np.arange(BLOCKS)[None, :]
    eye = np.eye(OWN)
    ahead = np.concatenate([np.kron(np.cos(coarse), eye), np.kron(-np.sin(coarse), eye)], axis=0)
    back = ahead.T / total
    turn = 2 * math.pi / total * low * np.arange(SPAN)[None, :]
    turn = np.repeat(turn, OWN, axis=0)
    fine = 2 * math.pi / SPAN * (np.arange(SPAN)[:, None] * np.arange(SPAN)[None, :] % SPAN)
    as_bf = lambda table: jnp.asarray(table.astype(np.float32)).astype(BF)
    return dict(
        ahead=as_bf(ahead),
        back=as_bf(back),
        fine=as_bf(np.concatenate([np.cos(fine), np.sin(fine)], axis=0)),
        turn=as_bf(np.concatenate([np.cos(turn), np.sin(turn)], axis=0)),
    )


def swap_halves(tiles):
    count, _, columns = tiles.shape
    pairs = tiles.reshape(count // 2, 2, 8, columns)
    first, second = pairs[:, 0], pairs[:, 1]
    upper = lax.broadcasted_iota(jnp.int32, first.shape, 1) < 4
    return (
        jnp.where(upper, first, pltpu.roll(second, 4, 1)),
        jnp.where(upper, pltpu.roll(first, 4, 1), second),
    )


def pack_kernel(projected_ref, filters_ref, taps_hbm, out_ref, rows_ref, rim_ref, long_ref, taps_ref, sent_ref, sems):
    parts = (
        (filters_ref, long_ref),
        (taps_hbm, taps_ref),
        (projected_ref.at[1], rows_ref.at[0]),
        (projected_ref.at[2], rows_ref.at[1]),
        (projected_ref.at[0, pl.ds(0, 16)], rim_ref.at[0]),
        (projected_ref.at[0, pl.ds(SPAN - 16, 16)], rim_ref.at[1]),
    )
    reads = [pltpu.make_async_copy(*part, sems.at[n]) for n, part in enumerate(parts)]
    for read in reads:
        read.start()

    def by_device(turned):
        columns = turned.shape[1]
        turned = turned.astype(F32).reshape(2, BLOCKS // 2, OWN, columns)
        both = jnp.stack([turned[0], turned[1]], axis=1).reshape(BLOCKS, OWN, columns)
        return jnp.stack(swap_halves(both), axis=1).reshape(BLOCKS, OWN, columns)

    def store(first_row, rows):
        both = by_device(rows.T)
        sent_ref[:, first_row : first_row + 16, :] = jnp.concatenate([both[:, :, :128], both[:, :, 128:]], axis=1).astype(BF)

    reads[0].wait()
    store(16, long_ref[...].astype(BF))
    for read in reads[1:]:
        read.wait()

    def shaped(which):
        rows = rows_ref[which].astype(F32)
        total = taps_ref[0, which + 1 : which + 2, :] * rows
        for tap in (1, 2):
            total = total + taps_ref[tap, which + 1 : which + 2, :] * pltpu.roll(rows, tap, 0)
        return total

    store(0, (shaped(0) * shaped(1)).astype(BF))
    key, value, query = rows_ref[0], rows_ref[1], rim_ref[...]
    first = [key[:16], value[:16], query[0]]
    last = [key[SPAN - 16 :], value[SPAN - 16 :], query[1]]
    first = [rows.astype(F32)[:2] for rows in first]
    last = [rows.astype(F32)[14:] for rows in last]
    blank = jnp.zeros((2, SPAN), F32)
    edges = jnp.concatenate(first + [blank] + last + [blank, jnp.zeros((112, SPAN), F32)], axis=0)
    sent_ref[:, 32:40, :] = by_device(edges.T).astype(BF)
    write = pltpu.make_async_copy(sent_ref, out_ref, sems.at[6])
    write.start()
    write.wait()


def query_kernel(projected_ref, taps_ref, *rest):
    *out_refs, rows_ref, sem = rest
    read = pltpu.make_async_copy(projected_ref.at[0], rows_ref, sem)
    read.start()
    place = lax.axis_index("chan")
    read.wait()
    rows = rows_ref[...].astype(F32)
    total = taps_ref[0, 0:1, :] * rows
    for tap in (1, 2):
        total = total + taps_ref[tap, 0:1, :] * pltpu.roll(rows, tap, 0)
    total = jnp.where(lax.broadcasted_iota(jnp.int32, (SPAN, SPAN), 0) < 2, 1.0, total)
    rows_ref[...] = total.astype(BF)
    for step, out_ref in enumerate(out_refs):
        block = lax.rem(place + 4 - step, 4)
        out_ref[...] = rows_ref[pl.ds(pl.multiple_of(64 * block, 64), 64), :]


def conv_kernel(got_ref, taps_ref, skip_ref, ahead_ref, fine_ref, turn_ref, back_ref, out_ref):
    place = lax.axis_index("seq")
    lane = lax.broadcasted_iota(jnp.int32, (OWN, SPAN), 1)
    row = lax.broadcasted_iota(jnp.int32, (OWN, SPAN), 0)
    mine = lane == 128 * (row >> 2) + 4 * place + (row & 3)

    def own(values):
        return jnp.sum(jnp.where(mine, values, 0.0), axis=1, keepdims=True)[None]

    def block(first_row):
        both = got_ref[:, first_row : first_row + 16, :].astype(F32)
        return both[:, :8], both[:, 8:]

    edges = got_ref[:, 32:40, :].astype(F32)
    before = jnp.concatenate([jnp.zeros((1, OWN, 128), F32), edges[:-1]], axis=0)
    thin = lax.broadcasted_iota(jnp.int32, (BLOCKS, OWN, 128), 2)

    def shaped(which):
        at = (4, 0, 2)[which]
        left = lambda rows, by: rows if by % 128 == 0 else pltpu.roll(rows, -by % 128, 2)
        now = left(edges, at)
        once = jnp.where(thin == 0, left(before, at + 9), left(edges, at - 1))
        twice = left(before, at + 8)
        gains = [own(taps_ref[tap, which : which + 1, :]) for tap in range(3)]
        return now * gains[0] + once * gains[1] + twice * gains[2]

    early, late = block(0)
    early = jnp.where(thin < 2, shaped(1) * shaped(2), early)
    signal = jnp.concatenate([early.reshape(SPAN, 128), late.reshape(SPAN, 128)], axis=1).astype(BF)
    response = jnp.concatenate([half.reshape(SPAN, 128) for half in block(16)], axis=1).astype(BF)
    res_half = dot(ahead_ref[...], response)
    sig_half = dot(ahead_ref[...], signal)
    cos, sin = turn_ref[:SPAN].astype(F32), turn_ref[SPAN:].astype(F32)
    fine_cos, fine_sin = fine_ref[:SPAN], fine_ref[SPAN:]
    fine_less = -fine_sin
    spread = jnp.concatenate(
        [jnp.concatenate([fine_cos, fine_less], axis=1), jnp.concatenate([fine_sin, fine_cos], axis=1)], axis=0
    )
    gather = jnp.concatenate(
        [jnp.concatenate([fine_cos, fine_sin], axis=1), jnp.concatenate([fine_less, fine_cos], axis=1)], axis=0
    )

    def spectrum(half):
        real, imag = half[:SPAN], half[SPAN:]
        turned = jnp.concatenate([real * cos + imag * sin, imag * cos - real * sin], axis=1)
        both = dot(turned.astype(BF), spread)
        return both[:, :SPAN], both[:, SPAN:]

    res_real, res_imag = spectrum(res_half)
    sig_real, sig_imag = spectrum(sig_half)
    product = jnp.concatenate(
        [sig_real * res_real - sig_imag * res_imag, sig_real * res_imag + sig_imag * res_real], axis=1
    )
    both = dot(product.astype(BF), gather)
    real, imag = both[:, :SPAN], both[:, SPAN:]
    turned = jnp.concatenate([real * cos - imag * sin, real * sin + imag * cos], axis=0)
    conv = dot(back_ref[...], turned.astype(BF))
    skip = own(skip_ref[...])
    direct = (signal.astype(F32).reshape(BLOCKS, OWN, SPAN) * skip).reshape(SPAN, SPAN)
    mixed = (conv + direct).reshape(BLOCKS, OWN, SPAN)
    early = jnp.where(thin < 2, mixed[:, :, :128] * shaped(0), mixed[:, :, :128])
    halves = [[rows.reshape(128, 128) for rows in swap_halves(part)] for part in (early, mixed[:, :, 128:])]
    half = lax.broadcasted_iota(jnp.int32, (128, 128), 1) < 64
    for h in range(2):
        low, high = halves[h]
        even = jnp.where(half, low, pltpu.roll(high, 64, 1))
        odd = jnp.where(half, pltpu.roll(low, 64, 1), high)
        out_ref[256 * h : 256 * h + 128, :] = even.astype(BF)
        out_ref[256 * h + 128 : 256 * h + 256, :] = odd.astype(BF)


def project_kernel(got_ref, own_ref, near_ref, swap_ref, other_ref, far_ref, far_swap_ref, *rest):
    *query_refs, out_ref = rest
    place = lax.axis_index("chan")
    odd = lax.axis_index("seq") % 2

    def gated(step):
        owner = lax.rem(place + step, 4)
        rows = got_ref[pl.ds(pl.multiple_of(owner * 128, 128), 128), :].astype(F32).T
        return (jnp.concatenate([rows[:64], rows[64:]], axis=1) * query_refs[step][...].astype(F32)).astype(BF)

    blocks = [gated(step) for step in range(4)]
    total = dot(blocks[0], own_ref[...]) + dot(jnp.where(odd == 0, blocks[1], blocks[3]), near_ref[...])
    for rows, here_ref, there_ref in (
        (jnp.where(odd == 0, blocks[3], blocks[1]), other_ref, swap_ref),
        (blocks[2], far_ref, far_swap_ref),
    ):
        total = total + dot(jnp.where(odd == 0, rows[:, :128], rows[:, 128:]), here_ref[...])
        total = total + dot(jnp.where(odd == 0, rows[:, 128:], rows[:, :128]), there_ref[...])
    out_ref[...] = total.astype(BF)


HBM = pl.BlockSpec(memory_space=pltpu.HBM)
VMEM = pl.BlockSpec(memory_space=pltpu.VMEM)
PARAMS = pltpu.CompilerParams(vmem_limit_bytes=32 * 1024 * 1024)


TINY = pl.CostEstimate(flops=1000, bytes_accessed=1000, transcendentals=0)


def pack(projected, filters, short_taps):
    return pl.pallas_call(
        pack_kernel,
        out_shape=jax.ShapeDtypeStruct((BLOCKS, 40, 128), BF),
        in_specs=[HBM] * 3,
        out_specs=HBM,
        scratch_shapes=[
            pltpu.VMEM((2, SPAN, SPAN), BF),
            pltpu.VMEM((2, 16, SPAN), BF),
            pltpu.VMEM((SPAN, SPAN), F32),
            pltpu.VMEM((3, 3, SPAN), F32),
            pltpu.VMEM((BLOCKS, 40, 128), BF),
            pltpu.SemaphoreType.DMA((7,)),
        ],
        cost_estimate=TINY,
    )(projected, filters, short_taps)


def queries(projected, short_taps):
    return pl.pallas_call(
        query_kernel,
        out_shape=[jax.ShapeDtypeStruct((64, SPAN), BF)] * 4,
        in_specs=[HBM, VMEM],
        out_specs=[VMEM] * 4,
        scratch_shapes=[pltpu.VMEM((SPAN, SPAN), BF), pltpu.SemaphoreType.DMA],
        compiler_params=PARAMS,
        cost_estimate=TINY,
    )(projected, short_taps)


def convolve(got, short_taps, skip_gain):
    table = constants()
    held = [short_taps, skip_gain.reshape(1, SPAN)] + [table[name] for name in ("ahead", "fine", "turn", "back")]
    return pl.pallas_call(
        conv_kernel,
        out_shape=jax.ShapeDtypeStruct((512, 128), BF),
        in_specs=[VMEM] * 7,
        out_specs=VMEM,
        compiler_params=PARAMS,
        cost_estimate=TINY,
    )(got, *held)


def project(got, weights, query_blocks):
    return pl.pallas_call(
        project_kernel,
        out_shape=jax.ShapeDtypeStruct((64, 1024), BF),
        in_specs=[VMEM] * (1 + len(weights) + len(query_blocks)),
        out_specs=VMEM,
        compiler_params=PARAMS,
        cost_estimate=TINY,
    )(got, *weights, *query_blocks)


def on_device(projected, short_taps, filters, skip_gain, out_weight):
    ring = [(s * 4 + (j + (1 if s % 2 == 0 else 3)) % 4, s * 4 + j) for s in range(BLOCKS) for j in range(4)]
    pairs = [(s, s ^ 1) for s in range(BLOCKS)]
    near = lax.ppermute(out_weight, ("seq", "chan"), ring)
    core = lax.axis_index("seq") & 1
    half = lax.dynamic_slice_in_dim(near, 128 * core, 128, 0)
    other = lax.dynamic_slice_in_dim(near, 128 - 128 * core, 128, 0)
    far = lax.ppermute(half, ("seq", "chan"), ring)
    swaps = [lax.ppermute(part, "seq", pairs) for part in (half, other)]
    by_part = projected.transpose(1, 0, 2)
    got = lax.all_to_all(pack(by_part, filters, short_taps), "seq", split_axis=0, concat_axis=0, tiled=True)
    query_blocks = [
        block if step == 0 else lax.ppermute(block, "chan", [(j, (j - step) % 4) for j in range(4)])
        for step, block in enumerate(queries(by_part, short_taps))
    ]
    got, *swaps = lax.optimization_barrier((got, *swaps))
    mixed = convolve(got, short_taps, skip_gain)
    _, far = lax.optimization_barrier((mixed, far))
    weights = (out_weight, near, *swaps, far, lax.ppermute(far, "seq", pairs))
    got = lax.all_to_all(mixed.reshape(128, 4, 128), ("chan", "seq"), split_axis=0, concat_axis=0, tiled=True)
    return project(got.reshape(512, 128), weights, query_blocks)


def solution(mesh):
    return jax.shard_map(
        on_device,
        mesh=mesh,
        in_specs=(
            P("seq", None, "chan"),
            P(None, None, "chan"),
            P("seq", "chan"),
            P("chan"),
            P("chan", None),
        ),
        out_specs=P(("seq", "chan"), None),
        check_vma=False,
    )
```

```python
import math

import jax
import jax.numpy as jnp
import numpy as np
from jax import lax
from jax.experimental import pallas as pl
from jax.experimental.pallas import tpu as pltpu
from jax.sharding import PartitionSpec as P

BLOCKS = 32
SPAN = 256
OWN = 8
BF = jnp.bfloat16
F32 = jnp.float32


def dot(left, right):
    return jnp.dot(left, right, preferred_element_type=F32)


def constants():
    total = BLOCKS * SPAN
    low = np.arange(BLOCKS)[:, None] + 0.25
    coarse = 2 * math.pi / BLOCKS * low * np.arange(BLOCKS)[None, :]
    eye = np.eye(OWN)
    ahead = np.concatenate([np.kron(np.cos(coarse), eye), np.kron(-np.sin(coarse), eye)], axis=0)
    back = ahead.T / total
    turn = 2 * math.pi / total * low * np.arange(SPAN)[None, :]
    turn = np.repeat(turn, OWN, axis=0)
    fine = 2 * math.pi / SPAN * (np.arange(SPAN)[:, None] * np.arange(SPAN)[None, :] % SPAN)
    as_bf = lambda table: jnp.asarray(table.astype(np.float32)).astype(BF)
    return dict(
        ahead=as_bf(ahead),
        back=as_bf(back),
        fine=as_bf(np.concatenate([np.cos(fine), np.sin(fine)], axis=0)),
        turn=as_bf(np.concatenate([np.cos(turn), np.sin(turn)], axis=0)),
    )


def swap_halves(tiles):
    count, _, columns = tiles.shape
    pairs = tiles.reshape(count // 2, 2, 8, columns)
    first, second = pairs[:, 0], pairs[:, 1]
    upper = lax.broadcasted_iota(jnp.int32, first.shape, 1) < 4
    return (
        jnp.where(upper, first, pltpu.roll(second, 4, 1)),
        jnp.where(upper, pltpu.roll(first, 4, 1), second),
    )


def pack_kernel(projected_ref, filters_ref, taps_hbm, out_ref, rows_ref, rim_ref, long_ref, taps_ref, sent_ref, sems):
    parts = (
        (filters_ref, long_ref),
        (taps_hbm, taps_ref),
        (projected_ref.at[1], rows_ref.at[0]),
        (projected_ref.at[2], rows_ref.at[1]),
        (projected_ref.at[0, pl.ds(0, 16)], rim_ref.at[0]),
        (projected_ref.at[0, pl.ds(SPAN - 16, 16)], rim_ref.at[1]),
    )
    reads = [pltpu.make_async_copy(*part, sems.at[n]) for n, part in enumerate(parts)]
    for read in reads:
        read.start()

    def by_device(turned):
        columns = turned.shape[1]
        turned = turned.astype(F32).reshape(2, BLOCKS // 2, OWN, columns)
        both = jnp.stack([turned[0], turned[1]], axis=1).reshape(BLOCKS, OWN, columns)
        return jnp.stack(swap_halves(both), axis=1).reshape(BLOCKS, OWN, columns)

    def halves(rows):
        both = by_device(rows.T)
        return [both[:, :, :128], both[:, :, 128:]]

    reads[0].wait()
    long = halves(long_ref[...].astype(BF))
    for read in reads[1:]:
        read.wait()

    def shaped(which):
        rows = rows_ref[which].astype(F32)
        total = taps_ref[0, which + 1 : which + 2, :] * rows
        for tap in (1, 2):
            total = total + taps_ref[tap, which + 1 : which + 2, :] * pltpu.roll(rows, tap, 0)
        return total

    signal = halves((shaped(0) * shaped(1)).astype(BF))
    key, value, query = rows_ref[0], rows_ref[1], rim_ref[...]
    first = [key[:16], value[:16], query[0]]
    last = [key[SPAN - 16 :], value[SPAN - 16 :], query[1]]
    first = [rows.astype(F32)[:2] for rows in first]
    last = [rows.astype(F32)[14:] for rows in last]
    blank = jnp.zeros((2, SPAN), F32)
    edges = jnp.concatenate(first + [blank] + last + [blank, jnp.zeros((112, SPAN), F32)], axis=0)
    message = jnp.concatenate(signal + long + [by_device(edges.T)], axis=1)
    sent_ref[...] = message.reshape(BLOCKS * 40, 128).astype(BF)
    write = pltpu.make_async_copy(sent_ref, out_ref, sems.at[6])
    write.start()
    write.wait()


def query_kernel(projected_ref, taps_ref, *rest):
    *out_refs, rows_ref, sem = rest
    read = pltpu.make_async_copy(projected_ref.at[0], rows_ref, sem)
    read.start()
    place = lax.axis_index("chan")
    read.wait()
    rows = rows_ref[...].astype(F32)
    total = taps_ref[0, 0:1, :] * rows
    for tap in (1, 2):
        total = total + taps_ref[tap, 0:1, :] * pltpu.roll(rows, tap, 0)
    total = jnp.where(lax.broadcasted_iota(jnp.int32, (SPAN, SPAN), 0) < 2, 1.0, total)
    rows_ref[...] = total.astype(BF)
    for step, out_ref in enumerate(out_refs):
        block = lax.rem(place + 4 - step, 4)
        out_ref[...] = rows_ref[pl.ds(pl.multiple_of(64 * block, 64), 64), :]


def conv_kernel(got_ref, taps_ref, skip_ref, ahead_ref, fine_ref, turn_ref, back_ref, out_ref):
    place = lax.axis_index("seq")
    lane = lax.broadcasted_iota(jnp.int32, (OWN, SPAN), 1)
    row = lax.broadcasted_iota(jnp.int32, (OWN, SPAN), 0)
    mine = lane == 128 * (row >> 2) + 4 * place + (row & 3)

    def own(values):
        return jnp.sum(jnp.where(mine, values, 0.0), axis=1, keepdims=True)[None]

    got = got_ref[...].astype(F32).reshape(BLOCKS, 40, 128)

    def block(first_row):
        return got[:, first_row : first_row + 8], got[:, first_row + 8 : first_row + 16]

    edges = got[:, 32:40]
    before = jnp.concatenate([jnp.zeros((1, OWN, 128), F32), edges[:-1]], axis=0)
    thin = lax.broadcasted_iota(jnp.int32, (BLOCKS, OWN, 128), 2)

    def shaped(which):
        at = (4, 0, 2)[which]
        left = lambda rows, by: rows if by % 128 == 0 else pltpu.roll(rows, -by % 128, 2)
        now = left(edges, at)
        once = jnp.where(thin == 0, left(before, at + 9), left(edges, at - 1))
        twice = left(before, at + 8)
        gains = [own(taps_ref[tap, which : which + 1, :]) for tap in range(3)]
        return now * gains[0] + once * gains[1] + twice * gains[2]

    early, late = block(0)
    early = jnp.where(thin < 2, shaped(1) * shaped(2), early)
    signal = jnp.concatenate([early.reshape(SPAN, 128), late.reshape(SPAN, 128)], axis=1).astype(BF)
    response = jnp.concatenate([half.reshape(SPAN, 128) for half in block(16)], axis=1).astype(BF)
    res_half = dot(ahead_ref[...], response)
    sig_half = dot(ahead_ref[...], signal)
    cos, sin = turn_ref[:SPAN].astype(F32), turn_ref[SPAN:].astype(F32)
    fine_cos, fine_sin = fine_ref[:SPAN], fine_ref[SPAN:]
    fine_less = -fine_sin
    spread = jnp.concatenate(
        [jnp.concatenate([fine_cos, fine_less], axis=1), jnp.concatenate([fine_sin, fine_cos], axis=1)], axis=0
    )
    gather = jnp.concatenate(
        [jnp.concatenate([fine_cos, fine_sin], axis=1), jnp.concatenate([fine_less, fine_cos], axis=1)], axis=0
    )

    def spectrum(half):
        real, imag = half[:SPAN], half[SPAN:]
        turned = jnp.concatenate([real * cos + imag * sin, imag * cos - real * sin], axis=1)
        both = dot(turned.astype(BF), spread)
        return both[:, :SPAN], both[:, SPAN:]

    res_real, res_imag = spectrum(res_half)
    sig_real, sig_imag = spectrum(sig_half)
    product = jnp.concatenate(
        [sig_real * res_real - sig_imag * res_imag, sig_real * res_imag + sig_imag * res_real], axis=1
    )
    both = dot(product.astype(BF), gather)
    real, imag = both[:, :SPAN], both[:, SPAN:]
    turned = jnp.concatenate([real * cos - imag * sin, real * sin + imag * cos], axis=0)
    conv = dot(back_ref[...], turned.astype(BF))
    skip = own(skip_ref[...])
    direct = (signal.astype(F32).reshape(BLOCKS, OWN, SPAN) * skip).reshape(SPAN, SPAN)
    mixed = (conv + direct).reshape(BLOCKS, OWN, SPAN)
    early = jnp.where(thin < 2, mixed[:, :, :128] * shaped(0), mixed[:, :, :128])
    halves = [[rows.reshape(128, 128) for rows in swap_halves(part)] for part in (early, mixed[:, :, 128:])]
    half = lax.broadcasted_iota(jnp.int32, (128, 128), 1) < 64
    for h in range(2):
        low, high = halves[h]
        even = jnp.where(half, low, pltpu.roll(high, 64, 1))
        odd = jnp.where(half, pltpu.roll(low, 64, 1), high)
        out_ref[256 * h : 256 * h + 128, :] = even.astype(BF)
        out_ref[256 * h + 128 : 256 * h + 256, :] = odd.astype(BF)


def project_kernel(got_ref, own_ref, near_ref, swap_ref, other_ref, far_ref, far_swap_ref, *rest):
    *query_refs, out_ref = rest
    place = lax.axis_index("chan")
    odd = lax.axis_index("seq") % 2

    def gated(step):
        owner = lax.rem(place + step, 4)
        rows = got_ref[pl.ds(pl.multiple_of(owner * 128, 128), 128), :].astype(F32).T
        return (jnp.concatenate([rows[:64], rows[64:]], axis=1) * query_refs[step][...].astype(F32)).astype(BF)

    blocks = [gated(step) for step in range(4)]
    total = dot(blocks[0], own_ref[...]) + dot(jnp.where(odd == 0, blocks[1], blocks[3]), near_ref[...])
    for rows, here_ref, there_ref in (
        (jnp.where(odd == 0, blocks[3], blocks[1]), other_ref, swap_ref),
        (blocks[2], far_ref, far_swap_ref),
    ):
        total = total + dot(jnp.where(odd == 0, rows[:, :128], rows[:, 128:]), here_ref[...])
        total = total + dot(jnp.where(odd == 0, rows[:, 128:], rows[:, :128]), there_ref[...])
    out_ref[...] = total.astype(BF)


HBM = pl.BlockSpec(memory_space=pltpu.HBM)
VMEM = pl.BlockSpec(memory_space=pltpu.VMEM)
PARAMS = pltpu.CompilerParams(vmem_limit_bytes=32 * 1024 * 1024)


TINY = pl.CostEstimate(flops=1000, bytes_accessed=1000, transcendentals=0)


def pack(projected, filters, short_taps):
    return pl.pallas_call(
        pack_kernel,
        out_shape=jax.ShapeDtypeStruct((BLOCKS * 40, 128), BF),
        in_specs=[HBM] * 3,
        out_specs=HBM,
        scratch_shapes=[
            pltpu.VMEM((2, SPAN, SPAN), BF),
            pltpu.VMEM((2, 16, SPAN), BF),
            pltpu.VMEM((SPAN, SPAN), F32),
            pltpu.VMEM((3, 3, SPAN), F32),
            pltpu.VMEM((BLOCKS * 40, 128), BF),
            pltpu.SemaphoreType.DMA((7,)),
        ],
        cost_estimate=TINY,
    )(projected, filters, short_taps)


def queries(projected, short_taps):
    return pl.pallas_call(
        query_kernel,
        out_shape=[jax.ShapeDtypeStruct((64, SPAN), BF)] * 4,
        in_specs=[HBM, VMEM],
        out_specs=[VMEM] * 4,
        scratch_shapes=[pltpu.VMEM((SPAN, SPAN), BF), pltpu.SemaphoreType.DMA],
        compiler_params=PARAMS,
        cost_estimate=TINY,
    )(projected, short_taps)


def convolve(got, short_taps, skip_gain):
    table = constants()
    held = [short_taps, skip_gain.reshape(1, SPAN)] + [table[name] for name in ("ahead", "fine", "turn", "back")]
    return pl.pallas_call(
        conv_kernel,
        out_shape=jax.ShapeDtypeStruct((512, 128), BF),
        in_specs=[VMEM] * 7,
        out_specs=VMEM,
        compiler_params=PARAMS,
        cost_estimate=TINY,
    )(got, *held)


def project(got, weights, query_blocks):
    return pl.pallas_call(
        project_kernel,
        out_shape=jax.ShapeDtypeStruct((64, 1024), BF),
        in_specs=[VMEM] * (1 + len(weights) + len(query_blocks)),
        out_specs=VMEM,
        compiler_params=PARAMS,
        cost_estimate=TINY,
    )(got, *weights, *query_blocks)


def on_device(projected, short_taps, filters, skip_gain, out_weight):
    ring = [(s * 4 + (j + (1 if s % 2 == 0 else 3)) % 4, s * 4 + j) for s in range(BLOCKS) for j in range(4)]
    pairs = [(s, s ^ 1) for s in range(BLOCKS)]
    near = lax.ppermute(out_weight, ("seq", "chan"), ring)
    core = lax.axis_index("seq") & 1
    half = lax.dynamic_slice_in_dim(near, 128 * core, 128, 0)
    other = lax.dynamic_slice_in_dim(near, 128 - 128 * core, 128, 0)
    far = lax.ppermute(half, ("seq", "chan"), ring)
    swaps = [lax.ppermute(part, "seq", pairs) for part in (half, other)]
    by_part = projected.transpose(1, 0, 2)
    packed = pack(by_part, filters, short_taps).reshape(BLOCKS, 40, 128)
    got = lax.all_to_all(packed, "seq", split_axis=0, concat_axis=0, tiled=True).reshape(BLOCKS * 40, 128)
    query_blocks = [
        block if step == 0 else lax.ppermute(block, "chan", [(j, (j - step) % 4) for j in range(4)])
        for step, block in enumerate(queries(by_part, short_taps))
    ]
    got, *swaps = lax.optimization_barrier((got, *swaps))
    mixed = convolve(got, short_taps, skip_gain)
    _, far = lax.optimization_barrier((mixed, far))
    weights = (out_weight, near, *swaps, far, lax.ppermute(far, "seq", pairs))
    got = lax.all_to_all(mixed.reshape(128, 4, 128), ("chan", "seq"), split_axis=0, concat_axis=0, tiled=True)
    return project(got.reshape(512, 128), weights, query_blocks)


def solution(mesh):
    return jax.shard_map(
        on_device,
        mesh=mesh,
        in_specs=(
            P("seq", None, "chan"),
            P(None, None, "chan"),
            P("seq", "chan"),
            P("chan"),
            P("chan", None),
        ),
        out_specs=P(("seq", "chan"), None),
        check_vma=False,
    )
```

```python
import math

import jax
import jax.numpy as jnp
import numpy as np
from jax import lax
from jax.experimental import pallas as pl
from jax.experimental.pallas import tpu as pltpu
from jax.sharding import PartitionSpec as P

BLOCKS = 32
SPAN = 256
OWN = 8
BF = jnp.bfloat16
F32 = jnp.float32


def dot(left, right):
    return jnp.dot(left, right, preferred_element_type=F32)


def constants():
    total = BLOCKS * SPAN
    low = np.arange(BLOCKS)[:, None] + 0.25
    coarse = 2 * math.pi / BLOCKS * low * np.arange(BLOCKS)[None, :]
    eye = np.eye(OWN)
    ahead = np.concatenate([np.kron(np.cos(coarse), eye), np.kron(-np.sin(coarse), eye)], axis=0)
    back = ahead.T / total
    turn = 2 * math.pi / total * low * np.arange(SPAN)[None, :]
    turn = np.repeat(turn, OWN, axis=0)
    fine = 2 * math.pi / SPAN * (np.arange(SPAN)[:, None] * np.arange(SPAN)[None, :] % SPAN)
    as_bf = lambda table: jnp.asarray(table.astype(np.float32)).astype(BF)
    return dict(
        ahead=as_bf(ahead),
        back=as_bf(back),
        fine=as_bf(np.concatenate([np.cos(fine), np.sin(fine)], axis=0)),
        turn=as_bf(np.concatenate([np.cos(turn), np.sin(turn)], axis=0)),
    )


def swap_halves(tiles):
    count, _, columns = tiles.shape
    pairs = tiles.reshape(count // 2, 2, 8, columns)
    first, second = pairs[:, 0], pairs[:, 1]
    upper = lax.broadcasted_iota(jnp.int32, first.shape, 1) < 4
    return (
        jnp.where(upper, first, pltpu.roll(second, 4, 1)),
        jnp.where(upper, pltpu.roll(first, 4, 1), second),
    )


def pack_kernel(projected_ref, filters_ref, taps_hbm, out_ref, rows_ref, rim_ref, long_ref, taps_ref, sent_ref, sems):
    parts = (
        (filters_ref, long_ref),
        (taps_hbm, taps_ref),
        (projected_ref.at[1], rows_ref.at[0]),
        (projected_ref.at[2], rows_ref.at[1]),
        (projected_ref.at[0, pl.ds(0, 16)], rim_ref.at[0]),
        (projected_ref.at[0, pl.ds(SPAN - 16, 16)], rim_ref.at[1]),
    )
    reads = [pltpu.make_async_copy(*part, sems.at[n]) for n, part in enumerate(parts)]
    for read in reads:
        read.start()

    def by_device(turned):
        columns = turned.shape[1]
        turned = turned.astype(F32).reshape(2, BLOCKS // 2, OWN, columns)
        both = jnp.stack([turned[0], turned[1]], axis=1).reshape(BLOCKS, OWN, columns)
        return jnp.stack(swap_halves(both), axis=1).reshape(BLOCKS, OWN, columns)

    def halves(rows):
        both = by_device(rows.T)
        return [both[:, :, :128], both[:, :, 128:]]

    reads[0].wait()
    long = halves(long_ref[...].astype(BF))
    for read in reads[1:]:
        read.wait()

    def shaped(which):
        rows = rows_ref[which].astype(F32)
        total = taps_ref[0, which + 1 : which + 2, :] * rows
        for tap in (1, 2):
            total = total + taps_ref[tap, which + 1 : which + 2, :] * pltpu.roll(rows, tap, 0)
        return total

    signal = halves((shaped(0) * shaped(1)).astype(BF))
    key, value, query = rows_ref[0], rows_ref[1], rim_ref[...]
    first = [key[:16], value[:16], query[0]]
    last = [key[SPAN - 16 :], value[SPAN - 16 :], query[1]]
    first = [rows.astype(F32)[:2] for rows in first]
    last = [rows.astype(F32)[14:] for rows in last]
    blank = jnp.zeros((2, SPAN), F32)
    edges = jnp.concatenate(first + [blank] + last + [blank, jnp.zeros((112, SPAN), F32)], axis=0)
    message = jnp.concatenate(signal + long + [by_device(edges.T)], axis=1)
    sent_ref[...] = message.reshape(BLOCKS * 40, 128).astype(BF)
    write = pltpu.make_async_copy(sent_ref, out_ref, sems.at[6])
    write.start()
    write.wait()


def query_kernel(projected_ref, taps_ref, *rest):
    *out_refs, rows_ref, sem = rest
    read = pltpu.make_async_copy(projected_ref.at[0], rows_ref, sem)
    read.start()
    place = lax.axis_index("chan")
    read.wait()
    rows = rows_ref[...].astype(F32)
    total = taps_ref[0, 0:1, :] * rows
    for tap in (1, 2):
        total = total + taps_ref[tap, 0:1, :] * pltpu.roll(rows, tap, 0)
    total = jnp.where(lax.broadcasted_iota(jnp.int32, (SPAN, SPAN), 0) < 2, 1.0, total)
    rows_ref[...] = total.astype(BF)
    for step, out_ref in enumerate(out_refs):
        block = lax.rem(place + 4 - step, 4)
        out_ref[...] = rows_ref[pl.ds(pl.multiple_of(64 * block, 64), 64), :]


def conv_kernel(got_ref, taps_ref, skip_ref, ahead_ref, fine_ref, turn_ref, back_ref, out_ref, sent_ref, sems):
    place = lax.axis_index("seq")
    lane = lax.broadcasted_iota(jnp.int32, (OWN, SPAN), 1)
    row = lax.broadcasted_iota(jnp.int32, (OWN, SPAN), 0)
    mine = lane == 128 * (row >> 2) + 4 * place + (row & 3)

    def own(values):
        return jnp.sum(jnp.where(mine, values, 0.0), axis=1, keepdims=True)[None]

    got = got_ref[...].astype(F32).reshape(BLOCKS, 40, 128)

    def block(first_row):
        return got[:, first_row : first_row + 8], got[:, first_row + 8 : first_row + 16]

    edges = got[:, 32:40]
    before = jnp.concatenate([jnp.zeros((1, OWN, 128), F32), edges[:-1]], axis=0)
    thin = lax.broadcasted_iota(jnp.int32, (BLOCKS, OWN, 128), 2)

    def shaped(which):
        at = (4, 0, 2)[which]
        left = lambda rows, by: rows if by % 128 == 0 else pltpu.roll(rows, -by % 128, 2)
        now = left(edges, at)
        once = jnp.where(thin == 0, left(before, at + 9), left(edges, at - 1))
        twice = left(before, at + 8)
        gains = [own(taps_ref[tap, which : which + 1, :]) for tap in range(3)]
        return now * gains[0] + once * gains[1] + twice * gains[2]

    early, late = block(0)
    early = jnp.where(thin < 2, shaped(1) * shaped(2), early)
    signal = jnp.concatenate([early.reshape(SPAN, 128), late.reshape(SPAN, 128)], axis=1).astype(BF)
    response = jnp.concatenate([half.reshape(SPAN, 128) for half in block(16)], axis=1).astype(BF)
    res_half = dot(ahead_ref[...], response)
    sig_half = dot(ahead_ref[...], signal)
    cos, sin = turn_ref[:SPAN].astype(F32), turn_ref[SPAN:].astype(F32)
    fine_cos, fine_sin = fine_ref[:SPAN], fine_ref[SPAN:]
    fine_less = -fine_sin
    spread = jnp.concatenate(
        [jnp.concatenate([fine_cos, fine_less], axis=1), jnp.concatenate([fine_sin, fine_cos], axis=1)], axis=0
    )
    gather = jnp.concatenate(
        [jnp.concatenate([fine_cos, fine_sin], axis=1), jnp.concatenate([fine_less, fine_cos], axis=1)], axis=0
    )

    def spectrum(half):
        real, imag = half[:SPAN], half[SPAN:]
        turned = jnp.concatenate([real * cos + imag * sin, imag * cos - real * sin], axis=1)
        both = dot(turned.astype(BF), spread)
        return both[:, :SPAN], both[:, SPAN:]

    res_real, res_imag = spectrum(res_half)
    sig_real, sig_imag = spectrum(sig_half)
    product = jnp.concatenate(
        [sig_real * res_real - sig_imag * res_imag, sig_real * res_imag + sig_imag * res_real], axis=1
    )
    both = dot(product.astype(BF), gather)
    real, imag = both[:, :SPAN], both[:, SPAN:]
    turned = jnp.concatenate([real * cos - imag * sin, real * sin + imag * cos], axis=0)
    turned = turned.astype(BF)
    skip = own(skip_ref[...])
    half = lax.broadcasted_iota(jnp.int32, (128, 128), 1) < 64
    writes = []
    for h in range(2):
        columns = slice(128 * h, 128 * h + 128)
        conv = dot(back_ref[...], turned[:, columns]).reshape(BLOCKS, OWN, 128)
        part = conv + signal[:, columns].astype(F32).reshape(BLOCKS, OWN, 128) * skip
        if h == 0:
            part = jnp.where(thin < 2, part * shaped(0), part)
        low, high = (rows.reshape(128, 128) for rows in swap_halves(part))
        even = jnp.where(half, low, pltpu.roll(high, 64, 1))
        odd = jnp.where(half, pltpu.roll(low, 64, 1), high)
        sent_ref[256 * h : 256 * h + 256, :] = jnp.concatenate([even, odd], axis=0).astype(BF)
        rows = pl.ds(256 * h, 256)
        writes.append(pltpu.make_async_copy(sent_ref.at[rows], out_ref.at[rows], sems.at[h]))
        writes[h].start()
    for write in writes:
        write.wait()


def project_kernel(got_ref, own_ref, near_ref, swap_ref, other_ref, far_ref, far_swap_ref, *rest):
    *query_refs, out_ref = rest
    place = lax.axis_index("chan")
    odd = lax.axis_index("seq") % 2

    def gated(step):
        owner = lax.rem(place + step, 4)
        rows = got_ref[pl.ds(pl.multiple_of(owner * 128, 128), 128), :].astype(F32).T
        return (jnp.concatenate([rows[:64], rows[64:]], axis=1) * query_refs[step][...].astype(F32)).astype(BF)

    blocks = [gated(step) for step in range(4)]
    turned = (odd + place) % 2
    total = dot(blocks[0], own_ref[...]) + dot(jnp.where(turned == 0, blocks[1], blocks[3]), near_ref[...])
    for rows, here_ref, there_ref in (
        (jnp.where(turned == 0, blocks[3], blocks[1]), other_ref, swap_ref),
        (blocks[2], far_ref, far_swap_ref),
    ):
        total = total + dot(jnp.where(odd == 0, rows[:, :128], rows[:, 128:]), here_ref[...])
        total = total + dot(jnp.where(odd == 0, rows[:, 128:], rows[:, :128]), there_ref[...])
    out_ref[...] = total.astype(BF)


HBM = pl.BlockSpec(memory_space=pltpu.HBM)
VMEM = pl.BlockSpec(memory_space=pltpu.VMEM)
PARAMS = pltpu.CompilerParams(vmem_limit_bytes=32 * 1024 * 1024)


TINY = pl.CostEstimate(flops=1000, bytes_accessed=1000, transcendentals=0)


def pack(projected, filters, short_taps):
    return pl.pallas_call(
        pack_kernel,
        out_shape=jax.ShapeDtypeStruct((BLOCKS * 40, 128), BF),
        in_specs=[HBM] * 3,
        out_specs=HBM,
        scratch_shapes=[
            pltpu.VMEM((2, SPAN, SPAN), BF),
            pltpu.VMEM((2, 16, SPAN), BF),
            pltpu.VMEM((SPAN, SPAN), F32),
            pltpu.VMEM((3, 3, SPAN), F32),
            pltpu.VMEM((BLOCKS * 40, 128), BF),
            pltpu.SemaphoreType.DMA((7,)),
        ],
        cost_estimate=TINY,
    )(projected, filters, short_taps)


def queries(projected, short_taps):
    return pl.pallas_call(
        query_kernel,
        out_shape=[jax.ShapeDtypeStruct((64, SPAN), BF)] * 4,
        in_specs=[HBM, VMEM],
        out_specs=[VMEM] * 4,
        scratch_shapes=[pltpu.VMEM((SPAN, SPAN), BF), pltpu.SemaphoreType.DMA],
        compiler_params=PARAMS,
        cost_estimate=TINY,
    )(projected, short_taps)


def convolve(got, short_taps, skip_gain):
    table = constants()
    held = [short_taps, skip_gain.reshape(1, SPAN)] + [table[name] for name in ("ahead", "fine", "turn", "back")]
    return pl.pallas_call(
        conv_kernel,
        out_shape=jax.ShapeDtypeStruct((512, 128), BF),
        in_specs=[VMEM] * 7,
        out_specs=HBM,
        scratch_shapes=[pltpu.VMEM((512, 128), BF), pltpu.SemaphoreType.DMA((2,))],
        compiler_params=PARAMS,
        cost_estimate=TINY,
    )(got, *held)


def project(got, weights, query_blocks):
    return pl.pallas_call(
        project_kernel,
        out_shape=jax.ShapeDtypeStruct((64, 1024), BF),
        in_specs=[VMEM] * (1 + len(weights) + len(query_blocks)),
        out_specs=VMEM,
        compiler_params=PARAMS,
        cost_estimate=TINY,
    )(got, *weights, *query_blocks)


def on_device(projected, short_taps, filters, skip_gain, out_weight):
    pairs = [(s, s ^ 1) for s in range(BLOCKS)]
    fetch = [(s * 4 + (3 - j if s % 2 else j ^ 1), s * 4 + j) for s in range(BLOCKS) for j in range(4)]
    forward = [((s ^ 1) * 4 + (3 - j if s % 2 else j ^ 1), s * 4 + j) for s in range(BLOCKS) for j in range(4)]
    near = lax.ppermute(out_weight, ("seq", "chan"), fetch)
    core = lax.axis_index("seq") & 1
    passed = lax.dynamic_slice_in_dim(near, 128 - 128 * core, 128, 0)
    far = lax.ppermute(passed, ("seq", "chan"), forward)
    kept = lax.dynamic_slice_in_dim(near, 128 * core, 128, 0)
    swaps = [lax.ppermute(part, "seq", pairs) for part in (kept, passed)]
    by_part = projected.transpose(1, 0, 2)
    packed = pack(by_part, filters, short_taps).reshape(BLOCKS, 40, 128)
    got = lax.all_to_all(packed, "seq", split_axis=0, concat_axis=0, tiled=True).reshape(BLOCKS * 40, 128)
    query_blocks = [
        block if step == 0 else lax.ppermute(block, "chan", [(j, (j - step) % 4) for j in range(4)])
        for step, block in enumerate(queries(by_part, short_taps))
    ]
    got, *swaps = lax.optimization_barrier((got, *swaps))
    mixed = convolve(got, short_taps, skip_gain)
    _, far = lax.optimization_barrier((mixed, far))
    weights = (out_weight, near, *swaps, far, lax.ppermute(far, "seq", pairs))
    got = lax.all_to_all(mixed.reshape(128, 4, 128), ("chan", "seq"), split_axis=0, concat_axis=0, tiled=True)
    return project(got.reshape(512, 128), weights, query_blocks)


def solution(mesh):
    return jax.shard_map(
        on_device,
        mesh=mesh,
        in_specs=(
            P("seq", None, "chan"),
            P(None, None, "chan"),
            P("seq", "chan"),
            P("chan"),
            P("chan", None),
        ),
        out_specs=P(("seq", "chan"), None),
        check_vma=False,
    )
```

```python
import math

import jax
import jax.numpy as jnp
import numpy as np
from jax import lax
from jax.experimental import pallas as pl
from jax.experimental.pallas import tpu as pltpu
from jax.sharding import PartitionSpec as P

BLOCKS = 32
SPAN = 256
OWN = 8
BF = jnp.bfloat16
F32 = jnp.float32


def dot(left, right):
    return jnp.dot(left, right, preferred_element_type=F32)


def constants():
    total = BLOCKS * SPAN
    low = np.arange(BLOCKS)[:, None] + 0.25
    coarse = 2 * math.pi / BLOCKS * low * np.arange(BLOCKS)[None, :]
    eye = np.eye(OWN)
    ahead = np.concatenate([np.kron(np.cos(coarse), eye), np.kron(-np.sin(coarse), eye)], axis=0)
    back = ahead.T / total
    turn = 2 * math.pi / total * low * np.arange(SPAN)[None, :]
    turn = np.repeat(turn, OWN, axis=0)
    fine = 2 * math.pi / SPAN * (np.arange(SPAN)[:, None] * np.arange(SPAN)[None, :] % SPAN)
    as_bf = lambda table: jnp.asarray(table.astype(np.float32)).astype(BF)
    return dict(
        ahead=as_bf(ahead),
        back=as_bf(back),
        fine=as_bf(np.concatenate([np.cos(fine), np.sin(fine)], axis=0)),
        turn=as_bf(np.concatenate([np.cos(turn), np.sin(turn)], axis=0)),
    )


def swap_halves(tiles):
    count, _, columns = tiles.shape
    pairs = tiles.reshape(count // 2, 2, 8, columns)
    first, second = pairs[:, 0], pairs[:, 1]
    upper = lax.broadcasted_iota(jnp.int32, first.shape, 1) < 4
    return (
        jnp.where(upper, first, pltpu.roll(second, 4, 1)),
        jnp.where(upper, pltpu.roll(first, 4, 1), second),
    )


def pack_kernel(projected_ref, filters_ref, taps_hbm, out_ref, rows_ref, rim_ref, long_ref, taps_ref, sent_ref, sems):
    parts = (
        (filters_ref, long_ref),
        (taps_hbm, taps_ref),
        (projected_ref.at[1], rows_ref.at[0]),
        (projected_ref.at[2], rows_ref.at[1]),
        (projected_ref.at[0, pl.ds(0, 16)], rim_ref.at[0]),
        (projected_ref.at[0, pl.ds(SPAN - 16, 16)], rim_ref.at[1]),
    )
    reads = [pltpu.make_async_copy(*part, sems.at[n]) for n, part in enumerate(parts)]
    for read in reads:
        read.start()

    def by_device(turned):
        columns = turned.shape[1]
        turned = turned.astype(F32).reshape(2, BLOCKS // 2, OWN, columns)
        both = jnp.stack([turned[0], turned[1]], axis=1).reshape(BLOCKS, OWN, columns)
        return jnp.stack(swap_halves(both), axis=1).reshape(BLOCKS, OWN, columns)

    def halves(rows):
        both = by_device(rows.T)
        return [both[:, :, :128], both[:, :, 128:]]

    reads[0].wait()
    long = halves(long_ref[...].astype(BF))
    for read in reads[1:]:
        read.wait()

    def shaped(which):
        rows = rows_ref[which].astype(F32)
        total = taps_ref[0, which + 1 : which + 2, :] * rows
        for tap in (1, 2):
            total = total + taps_ref[tap, which + 1 : which + 2, :] * pltpu.roll(rows, tap, 0)
        return total

    signal = halves((shaped(0) * shaped(1)).astype(BF))
    key, value, query = rows_ref[0], rows_ref[1], rim_ref[...]
    first = [key[:16], value[:16], query[0]]
    last = [key[SPAN - 16 :], value[SPAN - 16 :], query[1]]
    first = [rows.astype(F32)[:2] for rows in first]
    last = [rows.astype(F32)[14:] for rows in last]
    blank = jnp.zeros((2, SPAN), F32)
    edges = jnp.concatenate(first + [blank] + last + [blank, jnp.zeros((112, SPAN), F32)], axis=0)
    message = jnp.concatenate(signal + long + [by_device(edges.T)], axis=1)
    writes = []
    for part in range(2):
        rows = pl.ds(640 * part, 640)
        sent_ref[640 * part : 640 * part + 640, :] = message[16 * part : 16 * part + 16].reshape(640, 128).astype(BF)
        writes.append(pltpu.make_async_copy(sent_ref.at[rows], out_ref.at[rows], sems.at[6 + part]))
        writes[part].start()
    for write in writes:
        write.wait()


def query_kernel(projected_ref, taps_ref, *rest):
    *out_refs, rows_ref, sem = rest
    read = pltpu.make_async_copy(projected_ref.at[0], rows_ref, sem)
    read.start()
    place = lax.axis_index("chan")
    read.wait()
    rows = rows_ref[...].astype(F32)
    total = taps_ref[0, 0:1, :] * rows
    for tap in (1, 2):
        total = total + taps_ref[tap, 0:1, :] * pltpu.roll(rows, tap, 0)
    total = jnp.where(lax.broadcasted_iota(jnp.int32, (SPAN, SPAN), 0) < 2, 1.0, total)
    rows_ref[...] = total.astype(BF)
    for step, out_ref in enumerate(out_refs):
        block = lax.rem(place + 4 - step, 4)
        out_ref[...] = rows_ref[pl.ds(pl.multiple_of(64 * block, 64), 64), :]


def conv_kernel(got_ref, taps_ref, skip_ref, ahead_ref, fine_ref, turn_ref, back_ref, out_ref):
    place = lax.axis_index("seq")
    lane = lax.broadcasted_iota(jnp.int32, (OWN, SPAN), 1)
    row = lax.broadcasted_iota(jnp.int32, (OWN, SPAN), 0)
    mine = lane == 128 * (row >> 2) + 4 * place + (row & 3)

    def own(values):
        return jnp.sum(jnp.where(mine, values, 0.0), axis=1, keepdims=True)[None]

    got = got_ref[...].astype(F32).reshape(BLOCKS, 40, 128)

    def block(first_row):
        return got[:, first_row : first_row + 8], got[:, first_row + 8 : first_row + 16]

    edges = got[:, 32:40]
    before = jnp.concatenate([jnp.zeros((1, OWN, 128), F32), edges[:-1]], axis=0)
    thin = lax.broadcasted_iota(jnp.int32, (BLOCKS, OWN, 128), 2)

    def shaped(which):
        at = (4, 0, 2)[which]
        left = lambda rows, by: rows if by % 128 == 0 else pltpu.roll(rows, -by % 128, 2)
        now = left(edges, at)
        once = jnp.where(thin == 0, left(before, at + 9), left(edges, at - 1))
        twice = left(before, at + 8)
        gains = [own(taps_ref[tap, which : which + 1, :]) for tap in range(3)]
        return now * gains[0] + once * gains[1] + twice * gains[2]

    early, late = block(0)
    early = jnp.where(thin < 2, shaped(1) * shaped(2), early)
    signal = jnp.concatenate([early.reshape(SPAN, 128), late.reshape(SPAN, 128)], axis=1).astype(BF)
    response = jnp.concatenate([half.reshape(SPAN, 128) for half in block(16)], axis=1).astype(BF)
    res_half = dot(ahead_ref[...], response)
    sig_half = dot(ahead_ref[...], signal)
    cos, sin = turn_ref[:SPAN].astype(F32), turn_ref[SPAN:].astype(F32)
    fine_cos, fine_sin = fine_ref[:SPAN], fine_ref[SPAN:]
    fine_less = -fine_sin
    spread = jnp.concatenate(
        [jnp.concatenate([fine_cos, fine_less], axis=1), jnp.concatenate([fine_sin, fine_cos], axis=1)], axis=0
    )
    gather = jnp.concatenate(
        [jnp.concatenate([fine_cos, fine_sin], axis=1), jnp.concatenate([fine_less, fine_cos], axis=1)], axis=0
    )

    def spectrum(half):
        real, imag = half[:SPAN], half[SPAN:]
        turned = jnp.concatenate([real * cos + imag * sin, imag * cos - real * sin], axis=1)
        both = dot(turned.astype(BF), spread)
        return both[:, :SPAN], both[:, SPAN:]

    res_real, res_imag = spectrum(res_half)
    sig_real, sig_imag = spectrum(sig_half)
    product = jnp.concatenate(
        [sig_real * res_real - sig_imag * res_imag, sig_real * res_imag + sig_imag * res_real], axis=1
    )
    both = dot(product.astype(BF), gather)
    real, imag = both[:, :SPAN], both[:, SPAN:]
    turned = jnp.concatenate([real * cos - imag * sin, real * sin + imag * cos], axis=0)
    conv = dot(back_ref[...], turned.astype(BF))
    skip = own(skip_ref[...])
    direct = (signal.astype(F32).reshape(BLOCKS, OWN, SPAN) * skip).reshape(SPAN, SPAN)
    mixed = (conv + direct).reshape(BLOCKS, OWN, SPAN)
    early = jnp.where(thin < 2, mixed[:, :, :128] * shaped(0), mixed[:, :, :128])
    halves = [[rows.reshape(128, 128) for rows in swap_halves(part)] for part in (early, mixed[:, :, 128:])]
    half = lax.broadcasted_iota(jnp.int32, (128, 128), 1) < 64
    for h in range(2):
        low, high = halves[h]
        even = jnp.where(half, low, pltpu.roll(high, 64, 1))
        odd = jnp.where(half, pltpu.roll(low, 64, 1), high)
        out_ref[256 * h : 256 * h + 128, :] = even.astype(BF)
        out_ref[256 * h + 128 : 256 * h + 256, :] = odd.astype(BF)


def project_kernel(got_ref, own_ref, near_ref, swap_ref, other_ref, far_ref, far_swap_ref, *rest):
    *query_refs, out_ref = rest
    place = lax.axis_index("chan")
    odd = lax.axis_index("seq") % 2

    def gated(step):
        owner = lax.rem(place + step, 4)
        rows = got_ref[pl.ds(pl.multiple_of(owner * 128, 128), 128), :].astype(F32).T
        return (jnp.concatenate([rows[:64], rows[64:]], axis=1) * query_refs[step][...].astype(F32)).astype(BF)

    blocks = [gated(step) for step in range(4)]
    total = dot(blocks[0], own_ref[...]) + dot(jnp.where(odd == 0, blocks[1], blocks[3]), near_ref[...])
    for rows, here_ref, there_ref in (
        (jnp.where(odd == 0, blocks[3], blocks[1]), other_ref, swap_ref),
        (blocks[2], far_ref, far_swap_ref),
    ):
        total = total + dot(jnp.where(odd == 0, rows[:, :128], rows[:, 128:]), here_ref[...])
        total = total + dot(jnp.where(odd == 0, rows[:, 128:], rows[:, :128]), there_ref[...])
    out_ref[...] = total.astype(BF)


HBM = pl.BlockSpec(memory_space=pltpu.HBM)
VMEM = pl.BlockSpec(memory_space=pltpu.VMEM)
PARAMS = pltpu.CompilerParams(vmem_limit_bytes=32 * 1024 * 1024)


TINY = pl.CostEstimate(flops=1000, bytes_accessed=1000, transcendentals=0)


def pack(projected, filters, short_taps):
    return pl.pallas_call(
        pack_kernel,
        out_shape=jax.ShapeDtypeStruct((BLOCKS * 40, 128), BF),
        in_specs=[HBM] * 3,
        out_specs=HBM,
        scratch_shapes=[
            pltpu.VMEM((2, SPAN, SPAN), BF),
            pltpu.VMEM((2, 16, SPAN), BF),
            pltpu.VMEM((SPAN, SPAN), F32),
            pltpu.VMEM((3, 3, SPAN), F32),
            pltpu.VMEM((BLOCKS * 40, 128), BF),
            pltpu.SemaphoreType.DMA((8,)),
        ],
        cost_estimate=TINY,
    )(projected, filters, short_taps)


def queries(projected, short_taps):
    return pl.pallas_call(
        query_kernel,
        out_shape=[jax.ShapeDtypeStruct((64, SPAN), BF)] * 4,
        in_specs=[HBM, VMEM],
        out_specs=[VMEM] * 4,
        scratch_shapes=[pltpu.VMEM((SPAN, SPAN), BF), pltpu.SemaphoreType.DMA],
        compiler_params=PARAMS,
        cost_estimate=TINY,
    )(projected, short_taps)


def convolve(got, short_taps, skip_gain):
    table = constants()
    held = [short_taps, skip_gain.reshape(1, SPAN)] + [table[name] for name in ("ahead", "fine", "turn", "back")]
    return pl.pallas_call(
        conv_kernel,
        out_shape=jax.ShapeDtypeStruct((512, 128), BF),
        in_specs=[VMEM] * 7,
        out_specs=VMEM,
        compiler_params=PARAMS,
        cost_estimate=TINY,
    )(got, *held)


def project(got, weights, query_blocks):
    return pl.pallas_call(
        project_kernel,
        out_shape=jax.ShapeDtypeStruct((64, 1024), BF),
        in_specs=[VMEM] * (1 + len(weights) + len(query_blocks)),
        out_specs=VMEM,
        compiler_params=PARAMS,
        cost_estimate=TINY,
    )(got, *weights, *query_blocks)


def on_device(projected, short_taps, filters, skip_gain, out_weight):
    ring = [(s * 4 + (j + (1 if s % 2 == 0 else 3)) % 4, s * 4 + j) for s in range(BLOCKS) for j in range(4)]
    pairs = [(s, s ^ 1) for s in range(BLOCKS)]
    near = lax.ppermute(out_weight, ("seq", "chan"), ring)
    core = lax.axis_index("seq") & 1
    half = lax.dynamic_slice_in_dim(near, 128 * core, 128, 0)
    other = lax.dynamic_slice_in_dim(near, 128 - 128 * core, 128, 0)
    far = lax.ppermute(half, ("seq", "chan"), ring)
    swaps = [lax.ppermute(part, "seq", pairs) for part in (half, other)]
    by_part = projected.transpose(1, 0, 2)
    packed = pack(by_part, filters, short_taps).reshape(BLOCKS, 40, 128)
    got = lax.all_to_all(packed, "seq", split_axis=0, concat_axis=0, tiled=True).reshape(BLOCKS * 40, 128)
    query_blocks = [
        block if step == 0 else lax.ppermute(block, "chan", [(j, (j - step) % 4) for j in range(4)])
        for step, block in enumerate(queries(by_part, short_taps))
    ]
    got, *swaps = lax.optimization_barrier((got, *swaps))
    mixed = convolve(got, short_taps, skip_gain)
    _, far = lax.optimization_barrier((mixed, far))
    weights = (out_weight, near, *swaps, far, lax.ppermute(far, "seq", pairs))
    got = lax.all_to_all(mixed.reshape(128, 4, 128), ("chan", "seq"), split_axis=0, concat_axis=0, tiled=True)
    return project(got.reshape(512, 128), weights, query_blocks)


def solution(mesh):
    return jax.shard_map(
        on_device,
        mesh=mesh,
        in_specs=(
            P("seq", None, "chan"),
            P(None, None, "chan"),
            P("seq", "chan"),
            P("chan"),
            P("chan", None),
        ),
        out_specs=P(("seq", "chan"), None),
        check_vma=False,
    )
```

```python
import math

import jax
import jax.numpy as jnp
import numpy as np
from jax import lax
from jax.experimental import pallas as pl
from jax.experimental.pallas import tpu as pltpu
from jax.sharding import PartitionSpec as P

BLOCKS = 32
SPAN = 256
OWN = 8
BF = jnp.bfloat16
F32 = jnp.float32


def dot(left, right):
    return jnp.dot(left, right, preferred_element_type=F32)


def constants():
    total = BLOCKS * SPAN
    low = np.arange(BLOCKS)[:, None] + 0.25
    coarse = 2 * math.pi / BLOCKS * low * np.arange(BLOCKS)[None, :]
    eye = np.eye(OWN)
    ahead = np.concatenate([np.kron(np.cos(coarse), eye), np.kron(-np.sin(coarse), eye)], axis=0)
    back = ahead.T / total
    turn = 2 * math.pi / total * low * np.arange(SPAN)[None, :]
    turn = np.repeat(turn, OWN, axis=0)
    fine = 2 * math.pi / SPAN * (np.arange(SPAN)[:, None] * np.arange(SPAN)[None, :] % SPAN)
    as_bf = lambda table: jnp.asarray(table.astype(np.float32)).astype(BF)
    return dict(
        ahead=as_bf(ahead),
        back=as_bf(back),
        fine=as_bf(np.concatenate([np.cos(fine), np.sin(fine)], axis=0)),
        turn=as_bf(np.concatenate([np.cos(turn), np.sin(turn)], axis=0)),
    )


def swap_halves(tiles):
    count, _, columns = tiles.shape
    pairs = tiles.reshape(count // 2, 2, 8, columns)
    first, second = pairs[:, 0], pairs[:, 1]
    upper = lax.broadcasted_iota(jnp.int32, first.shape, 1) < 4
    return (
        jnp.where(upper, first, pltpu.roll(second, 4, 1)),
        jnp.where(upper, pltpu.roll(first, 4, 1), second),
    )


def pack_kernel(projected_ref, filters_ref, taps_hbm, out_ref, rows_ref, rim_ref, long_ref, taps_ref, sent_ref, sems):
    parts = (
        (filters_ref, long_ref),
        (taps_hbm, taps_ref),
        (projected_ref.at[1], rows_ref.at[0]),
        (projected_ref.at[2], rows_ref.at[1]),
        (projected_ref.at[0, pl.ds(0, 16)], rim_ref.at[0]),
        (projected_ref.at[0, pl.ds(SPAN - 16, 16)], rim_ref.at[1]),
    )
    reads = [pltpu.make_async_copy(*part, sems.at[n]) for n, part in enumerate(parts)]
    for read in reads:
        read.start()

    def by_device(turned):
        columns = turned.shape[1]
        turned = turned.astype(F32).reshape(2, BLOCKS // 2, OWN, columns)
        both = jnp.stack([turned[0], turned[1]], axis=1).reshape(BLOCKS, OWN, columns)
        return jnp.stack(swap_halves(both), axis=1).reshape(BLOCKS, OWN, columns)

    def halves(rows):
        both = by_device(rows.T)
        return [both[:, :, :128], both[:, :, 128:]]

    reads[0].wait()
    long = halves(long_ref[...].astype(BF))
    for read in reads[1:]:
        read.wait()

    def shaped(which):
        rows = rows_ref[which].astype(F32)
        total = taps_ref[0, which + 1 : which + 2, :] * rows
        for tap in (1, 2):
            total = total + taps_ref[tap, which + 1 : which + 2, :] * pltpu.roll(rows, tap, 0)
        return total

    signal = halves((shaped(0) * shaped(1)).astype(BF))
    key, value, query = rows_ref[0], rows_ref[1], rim_ref[...]
    first = [key[:16], value[:16], query[0]]
    last = [key[SPAN - 16 :], value[SPAN - 16 :], query[1]]
    first = [rows.astype(F32)[:2] for rows in first]
    last = [rows.astype(F32)[14:] for rows in last]
    blank = jnp.zeros((2, SPAN), F32)
    edges = jnp.concatenate(first + [blank] + last + [blank, jnp.zeros((112, SPAN), F32)], axis=0)
    message = jnp.concatenate(signal + long + [by_device(edges.T)], axis=1)
    sent_ref[...] = message.reshape(BLOCKS * 40, 128).astype(BF)
    write = pltpu.make_async_copy(sent_ref, out_ref, sems.at[6])
    write.start()
    write.wait()


def query_kernel(projected_ref, taps_ref, *rest):
    *out_refs, rows_ref, sem = rest
    read = pltpu.make_async_copy(projected_ref.at[0], rows_ref, sem)
    read.start()
    place = lax.axis_index("chan")
    read.wait()
    rows = rows_ref[...].astype(F32)
    total = taps_ref[0, 0:1, :] * rows
    for tap in (1, 2):
        total = total + taps_ref[tap, 0:1, :] * pltpu.roll(rows, tap, 0)
    total = jnp.where(lax.broadcasted_iota(jnp.int32, (SPAN, SPAN), 0) < 2, 1.0, total)
    rows_ref[...] = total.astype(BF)
    for step, out_ref in enumerate(out_refs):
        block = lax.rem(place + 4 - step, 4)
        out_ref[...] = rows_ref[pl.ds(pl.multiple_of(64 * block, 64), 64), :]


def conv_kernel(got_ref, taps_ref, skip_ref, ahead_ref, fine_ref, turn_ref, back_ref, out_ref):
    place = lax.axis_index("seq")
    lane = lax.broadcasted_iota(jnp.int32, (OWN, SPAN), 1)
    row = lax.broadcasted_iota(jnp.int32, (OWN, SPAN), 0)
    mine = lane == 128 * (row >> 2) + 4 * place + (row & 3)

    def own(values):
        return jnp.sum(jnp.where(mine, values, 0.0), axis=1, keepdims=True)[None]

    got = got_ref[...].astype(F32).reshape(BLOCKS, 40, 128)

    def block(first_row):
        return got[:, first_row : first_row + 8], got[:, first_row + 8 : first_row + 16]

    response = jnp.concatenate([half.reshape(SPAN, 128) for half in block(16)], axis=1).astype(BF)
    res_half = dot(ahead_ref[...], response)

    edges = got[:, 32:40]
    before = jnp.concatenate([jnp.zeros((1, OWN, 128), F32), edges[:-1]], axis=0)
    thin = lax.broadcasted_iota(jnp.int32, (BLOCKS, OWN, 128), 2)

    def shaped(which):
        at = (4, 0, 2)[which]
        left = lambda rows, by: rows if by % 128 == 0 else pltpu.roll(rows, -by % 128, 2)
        now = left(edges, at)
        once = jnp.where(thin == 0, left(before, at + 9), left(edges, at - 1))
        twice = left(before, at + 8)
        gains = [own(taps_ref[tap, which : which + 1, :]) for tap in range(3)]
        return now * gains[0] + once * gains[1] + twice * gains[2]

    early, late = block(0)
    early = jnp.where(thin < 2, shaped(1) * shaped(2), early)
    signal = jnp.concatenate([early.reshape(SPAN, 128), late.reshape(SPAN, 128)], axis=1).astype(BF)
    sig_half = dot(ahead_ref[...], signal)
    cos, sin = turn_ref[:SPAN].astype(F32), turn_ref[SPAN:].astype(F32)
    fine_cos, fine_sin = fine_ref[:SPAN], fine_ref[SPAN:]
    fine_less = -fine_sin
    spread = jnp.concatenate(
        [jnp.concatenate([fine_cos, fine_less], axis=1), jnp.concatenate([fine_sin, fine_cos], axis=1)], axis=0
    )
    gather = jnp.concatenate(
        [jnp.concatenate([fine_cos, fine_sin], axis=1), jnp.concatenate([fine_less, fine_cos], axis=1)], axis=0
    )

    def spectrum(half):
        real, imag = half[:SPAN], half[SPAN:]
        turned = jnp.concatenate([real * cos + imag * sin, imag * cos - real * sin], axis=1)
        both = dot(turned.astype(BF), spread)
        return both[:, :SPAN], both[:, SPAN:]

    res_real, res_imag = spectrum(res_half)
    sig_real, sig_imag = spectrum(sig_half)
    product = jnp.concatenate(
        [sig_real * res_real - sig_imag * res_imag, sig_real * res_imag + sig_imag * res_real], axis=1
    )
    both = dot(product.astype(BF), gather)
    real, imag = both[:, :SPAN], both[:, SPAN:]
    turned = jnp.concatenate([real * cos - imag * sin, real * sin + imag * cos], axis=0)
    conv = dot(back_ref[...], turned.astype(BF))
    skip = own(skip_ref[...])
    direct = (signal.astype(F32).reshape(BLOCKS, OWN, SPAN) * skip).reshape(SPAN, SPAN)
    mixed = (conv + direct).reshape(BLOCKS, OWN, SPAN)
    early = jnp.where(thin < 2, mixed[:, :, :128] * shaped(0), mixed[:, :, :128])
    halves = [[rows.reshape(128, 128) for rows in swap_halves(part)] for part in (early, mixed[:, :, 128:])]
    half = lax.broadcasted_iota(jnp.int32, (128, 128), 1) < 64
    for h in range(2):
        low, high = halves[h]
        even = jnp.where(half, low, pltpu.roll(high, 64, 1))
        odd = jnp.where(half, pltpu.roll(low, 64, 1), high)
        out_ref[256 * h : 256 * h + 128, :] = even.astype(BF)
        out_ref[256 * h + 128 : 256 * h + 256, :] = odd.astype(BF)


def project_kernel(got_ref, own_ref, near_ref, swap_ref, other_ref, far_ref, far_swap_ref, *rest):
    *query_refs, out_ref = rest
    place = lax.axis_index("chan")
    odd = lax.axis_index("seq") % 2

    def gated(step):
        owner = lax.rem(place + step, 4)
        rows = got_ref[pl.ds(pl.multiple_of(owner * 128, 128), 128), :].astype(F32).T
        return (jnp.concatenate([rows[:64], rows[64:]], axis=1) * query_refs[step][...].astype(F32)).astype(BF)

    blocks = [gated(step) for step in range(4)]
    total = dot(blocks[0], own_ref[...]) + dot(jnp.where(odd == 0, blocks[1], blocks[3]), near_ref[...])
    for rows, here_ref, there_ref in (
        (jnp.where(odd == 0, blocks[3], blocks[1]), other_ref, swap_ref),
        (blocks[2], far_ref, far_swap_ref),
    ):
        total = total + dot(jnp.where(odd == 0, rows[:, :128], rows[:, 128:]), here_ref[...])
        total = total + dot(jnp.where(odd == 0, rows[:, 128:], rows[:, :128]), there_ref[...])
    out_ref[...] = total.astype(BF)


HBM = pl.BlockSpec(memory_space=pltpu.HBM)
VMEM = pl.BlockSpec(memory_space=pltpu.VMEM)
PARAMS = pltpu.CompilerParams(vmem_limit_bytes=32 * 1024 * 1024)


TINY = pl.CostEstimate(flops=1000, bytes_accessed=1000, transcendentals=0)


def pack(projected, filters, short_taps):
    return pl.pallas_call(
        pack_kernel,
        out_shape=jax.ShapeDtypeStruct((BLOCKS * 40, 128), BF),
        in_specs=[HBM] * 3,
        out_specs=HBM,
        scratch_shapes=[
            pltpu.VMEM((2, SPAN, SPAN), BF),
            pltpu.VMEM((2, 16, SPAN), BF),
            pltpu.VMEM((SPAN, SPAN), F32),
            pltpu.VMEM((3, 3, SPAN), F32),
            pltpu.VMEM((BLOCKS * 40, 128), BF),
            pltpu.SemaphoreType.DMA((7,)),
        ],
        cost_estimate=TINY,
    )(projected, filters, short_taps)


def queries(projected, short_taps):
    return pl.pallas_call(
        query_kernel,
        out_shape=[jax.ShapeDtypeStruct((64, SPAN), BF)] * 4,
        in_specs=[HBM, VMEM],
        out_specs=[VMEM] * 4,
        scratch_shapes=[pltpu.VMEM((SPAN, SPAN), BF), pltpu.SemaphoreType.DMA],
        compiler_params=PARAMS,
        cost_estimate=TINY,
    )(projected, short_taps)


def convolve(got, short_taps, skip_gain):
    table = constants()
    held = [short_taps, skip_gain.reshape(1, SPAN)] + [table[name] for name in ("ahead", "fine", "turn", "back")]
    return pl.pallas_call(
        conv_kernel,
        out_shape=jax.ShapeDtypeStruct((512, 128), BF),
        in_specs=[VMEM] * 7,
        out_specs=VMEM,
        compiler_params=PARAMS,
        cost_estimate=TINY,
    )(got, *held)


def project(got, weights, query_blocks):
    return pl.pallas_call(
        project_kernel,
        out_shape=jax.ShapeDtypeStruct((64, 1024), BF),
        in_specs=[VMEM] * (1 + len(weights) + len(query_blocks)),
        out_specs=VMEM,
        compiler_params=PARAMS,
        cost_estimate=TINY,
    )(got, *weights, *query_blocks)


def on_device(projected, short_taps, filters, skip_gain, out_weight):
    ring = [(s * 4 + (j + (1 if s % 2 == 0 else 3)) % 4, s * 4 + j) for s in range(BLOCKS) for j in range(4)]
    pairs = [(s, s ^ 1) for s in range(BLOCKS)]
    near = lax.ppermute(out_weight, ("seq", "chan"), ring)
    core = lax.axis_index("seq") & 1
    half = lax.dynamic_slice_in_dim(near, 128 * core, 128, 0)
    other = lax.dynamic_slice_in_dim(near, 128 - 128 * core, 128, 0)
    far = lax.ppermute(half, ("seq", "chan"), ring)
    swaps = [lax.ppermute(part, "seq", pairs) for part in (half, other)]
    by_part = projected.transpose(1, 0, 2)
    packed = pack(by_part, filters, short_taps).reshape(BLOCKS, 40, 128)
    got = lax.all_to_all(packed, "seq", split_axis=0, concat_axis=0, tiled=True).reshape(BLOCKS * 40, 128)
    query_blocks = [
        block if step == 0 else lax.ppermute(block, "chan", [(j, (j - step) % 4) for j in range(4)])
        for step, block in enumerate(queries(by_part, short_taps))
    ]
    got, *swaps = lax.optimization_barrier((got, *swaps))
    mixed = convolve(got, short_taps, skip_gain)
    _, far = lax.optimization_barrier((mixed, far))
    weights = (out_weight, near, *swaps, far, lax.ppermute(far, "seq", pairs))
    got = lax.all_to_all(mixed.reshape(128, 4, 128), ("chan", "seq"), split_axis=0, concat_axis=0, tiled=True)
    return project(got.reshape(512, 128), weights, query_blocks)


def solution(mesh):
    return jax.shard_map(
        on_device,
        mesh=mesh,
        in_specs=(
            P("seq", None, "chan"),
            P(None, None, "chan"),
            P("seq", "chan"),
            P("chan"),
            P("chan", None),
        ),
        out_specs=P(("seq", "chan"), None),
        check_vma=False,
    )
```
